256 devices in a mesh: tile: 32 (over x, y, z_hi), fsdp: 8 (over z_lo, core).
Axes of the slice: x: 4, y: 4, z: 8 (z_hi: 2, z_lo: 4; z = z_hi * 4 + z_lo), core: 2. Of those that a mesh axis runs over, the one named last changes fastest.
Arguments:
- image: bfloat16 [128, 256, 640], P('tile', 'fsdp'), may hold values from -6 to 6
- conv_weight: bfloat16 [640, 9, 640], P('fsdp'), may hold values from -0.078125 to 0.078125
- group_weight: bfloat16 [9, 128, 640], P(None, None, 'fsdp'), may hold values from -0.1875 to 0.1875
- cotangent: bfloat16 [64, 128, 640], P('tile', 'fsdp'), may hold values from -6 to 6
Outputs:
- image_grad: bfloat16 [128, 256, 640], P('tile', 'fsdp')
- conv_weight_grad: float32 [640, 9, 640], P('fsdp', None, 'tile')
- group_weight_grad: float32 [9, 128, 640], P(None, 'fsdp', 'tile')
The draws below stay inside these ranges and needn't reach their ends.
All inputs are finite; a program needn't handle non-finite values.
Results may differ from the reference program's by a relative error of at most 0.0049.
Values may be sent and summed in bfloat16 or wider, within the bound.
No kernel may reach another device: no remote copies, remote signals or barrier semaphores. Data moves between devices by JAX's collectives and lax.ppermute only.
A program may use at most 64 MiB of HBM per device.

```python
import math
import jax
import jax.numpy as jnp
from jax import lax

CIN = 640
COUT = 640
CG = 128
GROUPS = 5
HOUT = 64
WOUT = 128
HIN = 128
WIN = 256


def spiked(array, own_key, source, target, blocks, factor):
    owner, partner = [(jnp.arange(array.shape[dim]) // (array.shape[dim] // blocks)).reshape([-1 if axis == dim else 1 for axis in range(array.ndim)]) for dim in (source, target)]
    chosen = jax.random.permutation(own_key, blocks)[partner]
    strong = (owner == chosen) | (owner == (partner + blocks // 2) % blocks)
    return jnp.where(strong, factor * array, array)


def level_of(rng, extent, split, smallest, top_value):
    gain, own = 1.0, jax.random.fold_in(rng, 6)
    for dim, shards_of in split:
        draws = jnp.exp(jax.random.uniform(jax.random.fold_in(own, dim), (shards_of,), jnp.float32, smallest / len(split), top_value / len(split)))
        gain = gain * jnp.repeat(draws, extent[dim] // shards_of).reshape([-1 if axis == dim else 1 for axis in range(len(extent))])
    return gain


def normal_values(rng, dims, width, limit, pieces=(), held_as=jnp.bfloat16):
    factor_of = level_of(rng, dims, pieces, -0.22, 0.18) if pieces else 1.0
    result = jax.random.normal(rng, dims, jnp.float32) * width * factor_of
    return jnp.minimum(jnp.maximum(result, -limit), limit).astype(held_as)


def noise_with(rng, extent, width, most, cuts, heavy, held_as=jnp.bfloat16):
    array = width * jax.random.normal(rng, extent, jnp.float32)
    if cuts:
        array = array * level_of(rng, extent, cuts, -0.22, 0.18)
    return jnp.clip(spiked(array, jax.random.fold_in(rng, 3), *heavy), -most, most).astype(held_as)


def setup_inputs(seed: int = 0) -> dict:
    key_list = jax.random.split(jax.random.key(seed), 5)
    image = noise_with(key_list[0], (HIN, WIN, CIN), 1.0, 6.0, ((0, 32), (1, 8)), (1, 2, 8, 2.0))
    conv_weight = normal_values(key_list[1], (CIN, 9, COUT), (9 * CIN) ** -0.5, 0.078125, ((0, 8),))
    group_weight = normal_values(key_list[2], (9, CG, COUT), (9 * CG) ** -0.5, 0.1875, ((2, 8),))
    cotangent = noise_with(key_list[3], (HOUT, WOUT, COUT), 1.0, 6.0, ((0, 32), (1, 8)), (0, 2, 32, 2.75))
    return dict(image=image, conv_weight=conv_weight, group_weight=group_weight, cotangent=cotangent)


def normal_terms(hidden_pre):
    cumul = 0.5 * (1.0 + lax.erf(hidden_pre * (1.0 / math.sqrt(2.0))))
    density = jnp.exp(-0.5 * hidden_pre * hidden_pre) * (1.0 / math.sqrt(2.0 * math.pi))
    return (cumul, density)

def reference(image, conv_weight, group_weight, cotangent):
    padded = jnp.pad(image, ((1, 0), (1, 0), (0, 0)))
    cells = HOUT * WOUT
    hidden_pre = jnp.zeros((cells, COUT), jnp.float32)
    for position in range(9):
        row_tap, col_tap = (position // 3, position % 3)
        window = padded[row_tap:row_tap + 2 * HOUT:2, col_tap:col_tap + 2 * WOUT:2].reshape(cells, CIN)
        hidden_pre = hidden_pre + jnp.dot(window, conv_weight[:, position, :], preferred_element_type=jnp.float32)
    hidden_pre = hidden_pre.reshape(HOUT, WOUT, COUT)
    cumul, density = normal_terms(hidden_pre)
    activation = (hidden_pre * cumul).astype(jnp.bfloat16)
    slopes = cumul + hidden_pre * density
    grad_pad = jnp.pad(cotangent, ((1, 1), (1, 1), (0, 0)))
    act_pad = jnp.pad(activation, ((1, 1), (1, 1), (0, 0)))
    weights_wide = group_weight.astype(jnp.float32).reshape(9, CG, GROUPS, CG)
    grad_groups = cotangent.astype(jnp.float32).reshape(cells, GROUPS, CG)
    act_grad = jnp.zeros((cells, GROUPS, CG), jnp.float32)
    group_terms = []
    for position in range(9):
        row_step, col_step = (position // 3 - 1, position % 3 - 1)
        moved = grad_pad[1 - row_step:1 - row_step + HOUT, 1 - col_step:1 - col_step + WOUT]
        moved = moved.astype(jnp.float32).reshape(cells, GROUPS, CG)
        act_grad = act_grad + jnp.einsum('pgj,igj->pgi', moved, weights_wide[position])
        shifted = act_pad[1 + row_step:1 + row_step + HOUT, 1 + col_step:1 + col_step + WOUT]
        shifted = shifted.astype(jnp.float32).reshape(cells, GROUPS, CG)
        group_terms.append(jnp.einsum('pgi,pgj->igj', shifted, grad_groups).reshape(CG, COUT))
    group_weight_grad = jnp.stack(group_terms, axis=0)
    pre_grad = (act_grad.reshape(HOUT, WOUT, COUT) * slopes).astype(jnp.bfloat16)
    grad_ext = jnp.pad(pre_grad, ((0, 1), (0, 1), (0, 0)))
    flat_grad = pre_grad.reshape(cells, COUT)
    parity = (1, 0, 1)
    offsets = (1, 0, 0)
    parts = [[jnp.zeros((cells, CIN), jnp.float32) for side in range(2)] for level in range(2)]
    conv_terms = []
    for position in range(9):
        row_tap, col_tap = (position // 3, position % 3)
        window = padded[row_tap:row_tap + 2 * HOUT:2, col_tap:col_tap + 2 * WOUT:2].reshape(cells, CIN)
        conv_terms.append(jnp.dot(window.T, flat_grad, preferred_element_type=jnp.float32))
        row_start, col_start = (offsets[row_tap], offsets[col_tap])
        source = grad_ext[row_start:row_start + HOUT, col_start:col_start + WOUT].reshape(cells, COUT)
        term = jnp.dot(source, conv_weight[:, position, :].T, preferred_element_type=jnp.float32)
        parts[parity[row_tap]][parity[col_tap]] = parts[parity[row_tap]][parity[col_tap]] + term
    conv_weight_grad = jnp.stack(conv_terms, axis=1)
    rounded = [[parts[level][side].astype(jnp.bfloat16).reshape(HOUT, WOUT, CIN) for side in range(2)] for level in range(2)]
    row_sets = [jnp.stack([rounded[level][0], rounded[level][1]], axis=2) for level in range(2)]
    image_grad = jnp.stack(row_sets, axis=1).reshape(2 * HOUT, 2 * WOUT, CIN)
    return (image_grad, conv_weight_grad, group_weight_grad)
```

```python
import functools
import math

import jax
import jax.numpy as jnp
from jax import lax
from jax.experimental import pallas as pl
from jax.experimental.pallas import tpu as pltpu
from jax.sharding import PartitionSpec as P

F32 = jnp.float32
BF16 = jnp.bfloat16
PARAMS = pltpu.CompilerParams(vmem_limit_bytes=48 * 1024 * 1024)


def nn(a, b):
    return lax.dot_general(a, b, (((1,), (0,)), ((), ())), preferred_element_type=F32)


def nt(a, b):
    return lax.dot_general(a, b, (((1,), (1,)), ((), ())), preferred_element_type=F32)


def tn(a, b):
    return lax.dot_general(a, b, (((0,), (0,)), ((), ())), preferred_element_type=F32)


def iota(shape, dim):
    return lax.broadcasted_iota(jnp.int32, shape, dim)


def from_left(x):
    return jnp.where(iota(x.shape, 1) == 0, 0.0, pltpu.roll(x, 1, 1))


def from_right(x):
    width = x.shape[1]
    return jnp.where(iota(x.shape, 1) == width - 1, 0.0, pltpu.roll(x, width - 1, 1))


def swap_blocks(arrays):
    arrays = list(arrays)
    lane = iota(arrays[0].shape, 1) // 16
    for step in (1, 2, 4):
        upper = (lane & step) != 0
        for low in range(8):
            if low & step:
                continue
            a, b = arrays[low], arrays[low | step]
            arrays[low] = jnp.where(upper, pltpu.roll(b, 16 * step, 1), a)
            arrays[low | step] = jnp.where(upper, b, pltpu.roll(a, 128 - 16 * step, 1))
    return arrays


def cell_of_lane(lane):
    return (lane // 32) * 32 + 2 * (lane % 16) + (lane // 16) % 2


def pack_kernel(image_ref, rim_ref, group_ref, cot_ref, send_ref):
    cells = jnp.concatenate([image_ref[...], rim_ref[...]], axis=0)
    lane = iota((160, 384), 1)
    pick = jnp.where((cell_of_lane(lane) == iota((160, 384), 0)) & (lane < 160), 1.0, 0.0)
    pixels = tn(cells, pick.astype(BF16))
    spread = jnp.where(iota((32, 256), 1) % 32 == iota((32, 256), 0), 1.0, 0.0)
    wide = tn(cot_ref[...], spread.astype(BF16))
    block = iota((80, 256), 1) // 32
    cot = wide[0:80]
    for b in range(1, 8):
        cot = jnp.where(block == b, wide[80 * b : 80 * b + 80], cot)
    cot = cot.astype(BF16)
    eye = jnp.where(iota((80, 80), 0) == iota((80, 80), 1), 1.0, 0.0).astype(BF16)
    above, below = jnp.zeros((160, 80), BF16), jnp.zeros((80, 80), BF16)
    for p in range(8):
        taps = [group_ref[t, 16 * p : 16 * p + 16, :] for t in range(9)]
        slab = nt(eye, jnp.concatenate([above, *taps, below], axis=0))
        send_ref[p, :, 0:384] = (pixels[80 * p : 80 * p + 80] + slab).astype(BF16)
        send_ref[p, :, 384:640] = cot


def forward_kernel(recv_ref, weight_ref, hid_ref, win_ref, own_ref, up_ref, down_ref, cot_ref, gw_ref):
    def tile(start):
        return swap_blocks([recv_ref[q, :, start : start + 128].astype(F32) for q in range(8)])

    inner = tile(0)
    rim = tile(128)
    even = [rim[0]] + [inner[2 * r] for r in range(4)]
    odd = [rim[1]] + [inner[2 * r + 1] for r in range(4)]
    left = [from_left(odd[r]).astype(BF16) for r in range(4)] + [None]
    even = [x.astype(BF16) for x in even]
    odd = [x.astype(BF16) for x in odd]
    for a in range(3):
        for b in range(3):
            t = 3 * a + b
            for i in range(2):
                r = 2 * i + a
                part = (left, even, odd)[b][r] if not (b == 0 and r == 4) else from_left(odd[4].astype(F32)).astype(BF16)
                win_ref[80 * t : 80 * t + 80, 128 * i : 128 * i + 128] = part
    hidden = tn(weight_ref[...], win_ref[...]).astype(BF16)
    for p in range(8):
        for g in range(5):
            hid_ref[p, 16 * g : 16 * g + 16, :] = hidden[128 * g + 16 * p : 128 * g + 16 * p + 16]
    for half in range(2):
        blocks = tile(384 + 128 * half)
        for k in range(8):
            b, i = 4 * half + k // 2, k % 2
            cot_ref[80 * b : 80 * b + 80, 128 * i : 128 * i + 128] = blocks[k].astype(BF16)
    for q in range(8):
        gw_ref[80 * q : 80 * q + 80, :] = recv_ref[q, :, 128:384]
    for g in range(5):
        rows = slice(128 * g, 128 * g + 128)
        terms = tn(gw_ref[rows, :], cot_ref[rows, :])
        sums = []
        for u in range(3):
            base = 32 + 48 * u
            by_row = []
            for i in range(2):
                lanes = slice(128 * i, 128 * i + 128)
                by_row.append(
                    from_right(terms[base : base + 16, lanes])
                    + terms[base + 16 : base + 32, lanes]
                    + from_left(terms[base + 32 : base + 48, lanes])
                )
            sums.append(by_row)
        here = slice(16 * g, 16 * g + 16)
        own_ref[here, 0:128] = sums[1][0] + sums[0][1]
        own_ref[here, 128:256] = sums[1][1] + sums[2][0]
        up_ref[here, :] = sums[0][0]
        down_ref[here, :] = sums[2][1]


def middle_kernel(hid_ref, own_ref, above_ref, below_ref, act_ref, pre_ref):
    hidden = hid_ref[0].astype(F32)
    for q in range(1, 8):
        hidden = hidden + hid_ref[q].astype(F32)
    cumul = 0.5 * (1.0 + lax.erf(hidden * (1.0 / math.sqrt(2.0))))
    density = jnp.exp(-0.5 * hidden * hidden) * (1.0 / math.sqrt(2.0 * math.pi))
    act_ref[...] = (hidden * cumul).astype(BF16)
    slopes = cumul + hidden * density
    act_grad = own_ref[...] + jnp.concatenate([above_ref[...], below_ref[...]], axis=1)
    pre_ref[...] = (act_grad * slopes).astype(BF16)


def backward_kernel(
    all_ref, weight_ref, win_ref, cot_ref, act_ref, above_ref, below_ref,
    img_ref, up_ref, red_ref, pre_ref, shift_ref,
):
    for p in range(8):
        for g in range(5):
            pre_ref[128 * g + 16 * p : 128 * g + 16 * p + 16, :] = all_ref[p, 16 * g : 16 * g + 16, :]
    pre = pre_ref[...]
    back = nn(weight_ref[...], pre)

    def term(a, b, i):
        t = 3 * a + b
        return back[80 * t : 80 * t + 80, 128 * i : 128 * i + 128]

    for i in range(2):
        img_ref[4 * i] = term(1, 1, i)
        img_ref[4 * i + 1] = term(1, 2, i) + from_right(term(1, 0, i))
    upper_even = [term(0, 1, i) for i in range(2)]
    upper_odd = [term(0, 2, i) + from_right(term(0, 0, i)) for i in range(2)]
    lower_odd = [term(2, 2, i) + from_right(term(2, 0, i)) for i in range(2)]
    img_ref[2] = term(2, 1, 0) + upper_even[1]
    img_ref[3] = lower_odd[0] + upper_odd[1]
    img_ref[6] = term(2, 1, 1)
    img_ref[7] = lower_odd[1]
    up_ref[0] = upper_even[0]
    up_ref[1] = upper_odd[0]

    red_ref[:, 0:640] = nt(pre, win_ref[0:640, :]).astype(BF16)
    rows = [above_ref[...].astype(F32), act_ref[:, 0:128].astype(F32), act_ref[:, 128:256].astype(F32), below_ref[...].astype(F32)]
    moved = [[from_left(x).astype(BF16) for x in rows], [x.astype(BF16) for x in rows], [from_right(x).astype(BF16) for x in rows]]
    for g in range(5):
        shift_ref[g, 0:80, :] = jnp.zeros((80, 256), BF16)
        shift_ref[g, 224:256, :] = jnp.zeros((32, 256), BF16)
        for u in range(3):
            for v in range(3):
                base = 80 + 16 * (3 * u + v)
                for i in range(2):
                    shift_ref[g, base : base + 16, 128 * i : 128 * i + 128] = moved[v][i + u][16 * g : 16 * g + 16]
    tail = jnp.concatenate([win_ref[640:720, :], jnp.zeros((176, 256), BF16)], axis=0)
    last = nt(pre, tail)
    for g in range(5):
        here = slice(128 * g, 128 * g + 128)
        red_ref[here, 640:896] = (last[here] + nt(cot_ref[here, :], shift_ref[g])).astype(BF16)


def fold_kernel(high_ref, red_ref, img_ref, below_ref, keep_ref, give_ref, send_ref):
    total = red_ref[0].astype(F32)
    for q in range(1, 16):
        total = total + red_ref[q].astype(F32)
    first, second = total[0:20], total[20:40]
    high = high_ref[0] == 1
    keep_ref[...] = jnp.where(high, second, first)
    give_ref[...] = jnp.where(high, first, second)
    parts = [img_ref[k] for k in range(8)]
    parts[6] = parts[6] + below_ref[0]
    parts[7] = parts[7] + below_ref[1]
    for q, x in enumerate(swap_blocks(parts)):
        send_ref[q] = x.astype(BF16)


def unpack_kernel(recv_ref, out_ref):
    lane = iota((128, 128), 1)
    pick = jnp.where(cell_of_lane(lane) == iota((128, 128), 0), 1.0, 0.0).astype(BF16)
    for p in range(5):
        out_ref[:, 128 * p : 128 * p + 128] = nt(pick, recv_ref[128 * p : 128 * p + 128, :]).astype(BF16)


def call(kernel, outs, *args, scratch=(), smem=0):
    whole = [pl.BlockSpec(memory_space=pltpu.SMEM)] * smem
    whole += [pl.BlockSpec(memory_space=pltpu.VMEM)] * (len(args) - smem)
    return pl.pallas_call(
        kernel,
        out_shape=[jax.ShapeDtypeStruct(shape, dtype) for shape, dtype in outs],
        in_specs=whole,
        out_specs=[pl.BlockSpec(memory_space=pltpu.VMEM)] * len(outs),
        scratch_shapes=list(scratch),
        compiler_params=PARAMS,
    )(*args)


def per_device(image, conv_weight, group_weight, cotangent):
    tiles = lax.axis_size("tile")
    downward = [(i, i + 1) for i in range(tiles - 1)]
    upward = [(i + 1, i) for i in range(tiles - 1)]
    partners = [(i, i ^ 1) for i in range(tiles)]
    planes = [[2 * i + z for i in range(tiles // 2)] for z in range(2)]

    rim = lax.ppermute(image[3:4], "tile", downward).reshape(32, 640)
    weights = conv_weight.transpose(1, 0, 2).reshape(720, 640)
    (send,) = call(
        pack_kernel, [((8, 80, 640), BF16)],
        image.reshape(128, 640), rim, group_weight, cotangent.reshape(32, 640),
    )
    recv = lax.all_to_all(send, "fsdp", 0, 0, tiled=True)
    hid, windows, own, up, down, cot = call(
        forward_kernel,
        [((8, 80, 256), BF16), ((720, 256), BF16), ((80, 256), F32), ((80, 128), F32), ((80, 128), F32), ((640, 256), BF16)],
        recv, weights,
        scratch=[pltpu.VMEM((640, 256), BF16)],
    )
    from_above = lax.ppermute(down, "tile", downward)
    from_below = lax.ppermute(up, "tile", upward)
    hid = lax.all_to_all(hid, "fsdp", 0, 0, tiled=True)
    act, pre = call(
        middle_kernel, [((80, 256), BF16), ((80, 256), BF16)], hid, own, from_above, from_below
    )
    act_above = lax.ppermute(act[:, 128:], "tile", downward)
    act_below = lax.ppermute(act[:, :128], "tile", upward)
    pre_all = lax.all_gather(pre, "fsdp", axis=0, tiled=False)
    img, img_up, red = call(
        backward_kernel,
        [((8, 80, 128), F32), ((2, 80, 128), F32), ((640, 896), BF16)],
        pre_all, weights, windows, cot, act, act_above, act_below,
        scratch=[pltpu.VMEM((640, 256), BF16), pltpu.VMEM((5, 256, 256), BF16)],
    )
    img_below = lax.ppermute(img_up, "tile", upward)
    red = lax.all_to_all(
        red.reshape(16, 40, 896), "tile", 0, 0, tiled=True, axis_index_groups=planes
    )
    high = (lax.axis_index("tile") % 2).astype(jnp.int32).reshape(1)
    keep, give, back = call(
        fold_kernel, [((20, 896), F32), ((20, 896), F32), ((8, 80, 128), BF16)],
        high, red, img, img_below, smem=1,
    )
    given = lax.ppermute(give, "tile", partners)
    back = lax.all_to_all(back, "fsdp", 0, 0, tiled=True)
    (image_grad,) = call(unpack_kernel, [((128, 640), BF16)], back.reshape(640, 128))
    total = keep + given
    conv_weight_grad = total[:, :720].reshape(20, 9, 80).transpose(2, 1, 0)
    group_weight_grad = total[:, 720:864].reshape(20, 9, 16).transpose(1, 2, 0)
    return (image_grad.reshape(4, 32, 640), conv_weight_grad, group_weight_grad)


def solution(mesh):
    placed = (
        P("tile", "fsdp", None),
        P("fsdp", None, None),
        P(None, None, "fsdp"),
        P("tile", "fsdp", None),
    )
    return jax.shard_map(
        per_device,
        mesh=mesh,
        in_specs=placed,
        out_specs=(P("tile", "fsdp", None), P("fsdp", None, "tile"), P(None, "fsdp", "tile")),
        check_vma=False,
    )
```

```python
import functools
import math

import jax
import jax.numpy as jnp
from jax import lax
from jax.experimental import pallas as pl
from jax.experimental.pallas import tpu as pltpu
from jax.sharding import PartitionSpec as P

F32 = jnp.float32
BF16 = jnp.bfloat16
PARAMS = pltpu.CompilerParams(vmem_limit_bytes=48 * 1024 * 1024)


def nn(a, b):
    return lax.dot_general(a, b, (((1,), (0,)), ((), ())), preferred_element_type=F32)


def nt(a, b):
    return lax.dot_general(a, b, (((1,), (1,)), ((), ())), preferred_element_type=F32)


def tn(a, b):
    return lax.dot_general(a, b, (((0,), (0,)), ((), ())), preferred_element_type=F32)


def iota(shape, dim):
    return lax.broadcasted_iota(jnp.int32, shape, dim)


def from_left(x):
    return jnp.where(iota(x.shape, 1) == 0, 0.0, pltpu.roll(x, 1, 1))


def from_right(x):
    width = x.shape[1]
    return jnp.where(iota(x.shape, 1) == width - 1, 0.0, pltpu.roll(x, width - 1, 1))


def swap_blocks(arrays):
    arrays = list(arrays)
    lane = iota(arrays[0].shape, 1) // 16
    for step in (1, 2, 4):
        upper = (lane & step) != 0
        for low in range(8):
            if low & step:
                continue
            a, b = arrays[low], arrays[low | step]
            arrays[low] = jnp.where(upper, pltpu.roll(b, 16 * step, 1), a)
            arrays[low | step] = jnp.where(upper, b, pltpu.roll(a, 128 - 16 * step, 1))
    return arrays


def cell_of_lane(lane):
    return (lane // 32) * 32 + 2 * (lane % 16) + (lane // 16) % 2


def pack_kernel(image_ref, group_ref, send_ref):
    pick = jnp.where(cell_of_lane(iota((128, 128), 1)) == iota((128, 128), 0), 1.0, 0.0)
    pixels = tn(image_ref[...], pick.astype(BF16)).astype(BF16)
    eye = jnp.where(iota((80, 80), 0) == iota((80, 80), 1), 1.0, 0.0).astype(BF16)
    above, below = jnp.zeros((32, 80), BF16), jnp.zeros((80, 80), BF16)
    for p in range(8):
        taps = [group_ref[t, 16 * p : 16 * p + 16, :] for t in range(9)]
        send_ref[p, :, 0:128] = pixels[80 * p : 80 * p + 80]
        send_ref[p, :, 128:384] = nt(eye, jnp.concatenate([above, *taps, below], axis=0)).astype(BF16)


def rim_kernel(base_ref, rim_ref, send_ref):
    lane = iota((32, 128), 1)
    pick = jnp.where((cell_of_lane(lane) == iota((32, 128), 0)) & (lane < 32), 1.0, 0.0)
    pixels = tn(rim_ref[...], pick.astype(BF16)).astype(BF16)
    here = iota((80, 128), 1) < 32
    for p in range(8):
        send_ref[p, :, 0:128] = base_ref[p, :, 0:128]
        send_ref[p, :, 128:256] = jnp.where(here, pixels[80 * p : 80 * p + 80], base_ref[p, :, 128:256])
        send_ref[p, :, 256:384] = base_ref[p, :, 256:384]


def forward_kernel(recv_ref, weight_ref, above_ref, cells_ref, below_ref, hid_ref, win_ref, share_ref):
    share_ref[0:16, :] = above_ref[...]
    share_ref[16:48, :] = cells_ref[...]
    share_ref[48:64, :] = below_ref[...]

    def tile(start):
        return swap_blocks([recv_ref[q, :, start : start + 128].astype(F32) for q in range(8)])

    inner = tile(0)
    rim = tile(128)
    even = [rim[0]] + [inner[2 * r] for r in range(4)]
    odd = [rim[1]] + [inner[2 * r + 1] for r in range(4)]
    left = [from_left(odd[r]).astype(BF16) for r in range(4)] + [None]
    even = [x.astype(BF16) for x in even]
    odd = [x.astype(BF16) for x in odd]
    for a in range(3):
        for b in range(3):
            t = 3 * a + b
            for i in range(2):
                r = 2 * i + a
                part = (left, even, odd)[b][r] if not (b == 0 and r == 4) else from_left(odd[4].astype(F32)).astype(BF16)
                win_ref[80 * t : 80 * t + 80, 128 * i : 128 * i + 128] = part
    hidden = tn(weight_ref[...], win_ref[...]).astype(BF16)
    for p in range(8):
        for g in range(5):
            hid_ref[p, 16 * g : 16 * g + 16, :] = hidden[128 * g + 16 * p : 128 * g + 16 * p + 16]


def group_kernel(recv_ref, all_ref, grad_ref, cot_ref, cell_ref, gw_ref):
    for q in range(8):
        gw_ref[80 * q : 80 * q + 80, :] = recv_ref[q, :, 128:384]
        for r in range(4):
            cell_ref[128 * r + 16 * q : 128 * r + 16 * q + 16, :] = all_ref[q, 16 * r : 16 * r + 16, :]
    eye = jnp.where(iota((128, 128), 0) == iota((128, 128), 1), 1.0, 0.0).astype(BF16)
    for g in range(5):
        rows = slice(128 * g, 128 * g + 128)
        cot = nt(eye, cell_ref[:, rows]).astype(BF16)
        cot_ref[rows, :] = cot
        terms = tn(gw_ref[rows, :], cot)
        for i in range(2):
            total = None
            for u in range(3):
                base = 32 + 48 * u
                lanes = slice(128 * (i + 2 - u), 128 * (i + 2 - u) + 128)
                part = (
                    from_right(terms[base : base + 16, lanes])
                    + terms[base + 16 : base + 32, lanes]
                    + from_left(terms[base + 32 : base + 48, lanes])
                )
                total = part if total is None else total + part
            grad_ref[16 * g : 16 * g + 16, 128 * i : 128 * i + 128] = total


def middle_kernel(hid_ref, grad_ref, act_ref, pre_ref):
    hidden = hid_ref[0].astype(F32)
    for q in range(1, 8):
        hidden = hidden + hid_ref[q].astype(F32)
    cumul = 0.5 * (1.0 + lax.erf(hidden * (1.0 / math.sqrt(2.0))))
    density = jnp.exp(-0.5 * hidden * hidden) * (1.0 / math.sqrt(2.0 * math.pi))
    act_ref[...] = (hidden * cumul).astype(BF16)
    slopes = cumul + hidden * density
    pre_ref[...] = (grad_ref[...] * slopes).astype(BF16)


def backward_kernel(
    all_ref, weight_ref, win_ref, cot_ref, act_ref, img_ref, up_ref, red_ref, pre_ref, shift_ref
):
    for p in range(8):
        for g in range(5):
            pre_ref[128 * g + 16 * p : 128 * g + 16 * p + 16, :] = all_ref[p, 16 * g : 16 * g + 16, :]
    pre = pre_ref[...]
    back = nn(weight_ref[...], pre)

    def term(a, b, i):
        t = 3 * a + b
        return back[80 * t : 80 * t + 80, 128 * i : 128 * i + 128]

    for i in range(2):
        img_ref[4 * i] = term(1, 1, i)
        img_ref[4 * i + 1] = term(1, 2, i) + from_right(term(1, 0, i))
    upper_even = [term(0, 1, i) for i in range(2)]
    upper_odd = [term(0, 2, i) + from_right(term(0, 0, i)) for i in range(2)]
    lower_odd = [term(2, 2, i) + from_right(term(2, 0, i)) for i in range(2)]
    img_ref[2] = term(2, 1, 0) + upper_even[1]
    img_ref[3] = lower_odd[0] + upper_odd[1]
    img_ref[6] = term(2, 1, 1)
    img_ref[7] = lower_odd[1]
    up_ref[0] = upper_even[0]
    up_ref[1] = upper_odd[0]

    red_ref[:, 0:640] = nt(pre, win_ref[0:640, :]).astype(BF16)
    rows = [act_ref[:, 128 * i : 128 * i + 128].astype(F32) for i in range(2)]
    moved = [[move(x).astype(BF16) for x in rows] for move in (from_left, lambda x: x, from_right)]
    shift_ref[...] = jnp.zeros((5, 256, 512), BF16)
    for g in range(5):
        for u in range(3):
            for v in range(3):
                base = 80 + 16 * (3 * u + v)
                for i in range(2):
                    lanes = slice(128 * (i + 2 - u), 128 * (i + 2 - u) + 128)
                    shift_ref[g, base : base + 16, lanes] = moved[v][i][16 * g : 16 * g + 16]
    tail = jnp.concatenate([win_ref[640:720, :], jnp.zeros((176, 256), BF16)], axis=0)
    last = nt(pre, tail)
    for g in range(5):
        here = slice(128 * g, 128 * g + 128)
        red_ref[here, 640:896] = (last[here] + nt(cot_ref[here, :], shift_ref[g])).astype(BF16)


def return_kernel(img_ref, below_ref, send_ref):
    parts = [img_ref[k] for k in range(8)]
    parts[6] = parts[6] + below_ref[0]
    parts[7] = parts[7] + below_ref[1]
    for q, x in enumerate(swap_blocks(parts)):
        send_ref[q] = x.astype(BF16)


def fold_kernel(high_ref, red_ref, keep_ref, give_ref):
    total = red_ref[0].astype(F32)
    for q in range(1, 16):
        total = total + red_ref[q].astype(F32)
    first, second = total[0:20], total[20:40]
    high = high_ref[0] == 1
    keep_ref[...] = jnp.where(high, second, first)
    give_ref[...] = jnp.where(high, first, second)


def unpack_kernel(recv_ref, out_ref):
    lane = iota((128, 128), 1)
    pick = jnp.where(cell_of_lane(lane) == iota((128, 128), 0), 1.0, 0.0).astype(BF16)
    for p in range(5):
        out_ref[:, 128 * p : 128 * p + 128] = nt(pick, recv_ref[128 * p : 128 * p + 128, :]).astype(BF16)


def finish_kernel(keep_ref, given_ref, conv_ref, group_ref):
    total = keep_ref[...] + given_ref[...]
    for t in range(9):
        conv_ref[t] = total[:, 80 * t : 80 * t + 80]
    group_ref[...] = jnp.transpose(total[:, 640:896])[80:224]


def call(kernel, outs, *args, scratch=(), smem=0):
    whole = [pl.BlockSpec(memory_space=pltpu.SMEM)] * smem
    whole += [pl.BlockSpec(memory_space=pltpu.VMEM)] * (len(args) - smem)
    return pl.pallas_call(
        kernel,
        out_shape=[jax.ShapeDtypeStruct(shape, dtype) for shape, dtype in outs],
        in_specs=whole,
        out_specs=[pl.BlockSpec(memory_space=pltpu.VMEM)] * len(outs),
        scratch_shapes=list(scratch),
        compiler_params=PARAMS,
    )(*args)


def per_device(image, conv_weight, group_weight, cotangent):
    tiles = lax.axis_size("tile")
    downward = [(i, i + 1) for i in range(tiles - 1)]
    upward = [(i + 1, i) for i in range(tiles - 1)]
    partners = [(i, i ^ 1) for i in range(tiles)]
    planes = [[2 * i + z for i in range(tiles // 2)] for z in range(2)]

    cells = cotangent.reshape(32, 640)
    rim = lax.ppermute(image[3:4], "tile", downward).reshape(32, 640)
    above = lax.ppermute(cotangent[1], "tile", downward)
    below = lax.ppermute(cotangent[0], "tile", upward)
    weights = conv_weight.transpose(1, 0, 2).reshape(720, 640)
    (base,) = call(pack_kernel, [((8, 80, 384), BF16)], image.reshape(128, 640), group_weight)
    (send,) = call(rim_kernel, [((8, 80, 384), BF16)], base, rim)
    recv = lax.all_to_all(send, "fsdp", 0, 0, tiled=True)
    hid, windows, share = call(
        forward_kernel,
        [((8, 80, 256), BF16), ((720, 256), BF16), ((64, 640), BF16)],
        recv, weights, above, cells, below,
    )
    cot_all = lax.all_gather(share, "fsdp", axis=0, tiled=False)
    grad, cot = call(
        group_kernel,
        [((80, 256), F32), ((640, 512), BF16)],
        recv, cot_all,
        scratch=[pltpu.VMEM((512, 640), BF16), pltpu.VMEM((640, 256), BF16)],
    )
    hid = lax.all_to_all(hid, "fsdp", 0, 0, tiled=True)
    act, pre = call(middle_kernel, [((80, 256), BF16), ((80, 256), BF16)], hid, grad)
    pre_all = lax.all_gather(pre, "fsdp", axis=0, tiled=False)
    img, img_up, red = call(
        backward_kernel,
        [((8, 80, 128), F32), ((2, 80, 128), F32), ((640, 896), BF16)],
        pre_all, weights, windows, cot, act,
        scratch=[pltpu.VMEM((640, 256), BF16), pltpu.VMEM((5, 256, 512), BF16)],
    )
    img_below = lax.ppermute(img_up, "tile", upward)
    red = lax.all_to_all(
        red.reshape(16, 40, 896), "tile", 0, 0, tiled=True, axis_index_groups=planes
    )
    (back,) = call(return_kernel, [((8, 80, 128), BF16)], img, img_below)
    back = lax.all_to_all(back, "fsdp", 0, 0, tiled=True)
    high = (lax.axis_index("tile") % 2).astype(jnp.int32).reshape(1)
    keep, give = call(fold_kernel, [((20, 896), F32), ((20, 896), F32)], high, red, smem=1)
    given = lax.ppermute(give, "tile", partners)
    (image_grad,) = call(unpack_kernel, [((128, 640), BF16)], back.reshape(640, 128))
    conv_weight_grad, group_weight_grad = call(
        finish_kernel, [((9, 20, 80), F32), ((144, 20), F32)], keep, given
    )
    conv_weight_grad = conv_weight_grad.transpose(2, 0, 1)
    group_weight_grad = group_weight_grad.reshape(9, 16, 20)
    return (image_grad.reshape(4, 32, 640), conv_weight_grad, group_weight_grad)


def solution(mesh):
    placed = (
        P("tile", "fsdp", None),
        P("fsdp", None, None),
        P(None, None, "fsdp"),
        P("tile", "fsdp", None),
    )
    return jax.shard_map(
        per_device,
        mesh=mesh,
        in_specs=placed,
        out_specs=(P("tile", "fsdp", None), P("fsdp", None, "tile"), P(None, "fsdp", "tile")),
        check_vma=False,
    )
```

```python
import functools
import math

import jax
import jax.numpy as jnp
from jax import lax
from jax.experimental import pallas as pl
from jax.experimental.pallas import tpu as pltpu
from jax.sharding import PartitionSpec as P

F32 = jnp.float32
BF16 = jnp.bfloat16
PARAMS = pltpu.CompilerParams(vmem_limit_bytes=48 * 1024 * 1024)


def nn(a, b):
    return lax.dot_general(a, b, (((1,), (0,)), ((), ())), preferred_element_type=F32)


def nt(a, b):
    return lax.dot_general(a, b, (((1,), (1,)), ((), ())), preferred_element_type=F32)


def tn(a, b):
    return lax.dot_general(a, b, (((0,), (0,)), ((), ())), preferred_element_type=F32)


def iota(shape, dim):
    return lax.broadcasted_iota(jnp.int32, shape, dim)


def from_left(x):
    return jnp.where(iota(x.shape, 1) == 0, 0.0, pltpu.roll(x, 1, 1))


def from_right(x):
    width = x.shape[1]
    return jnp.where(iota(x.shape, 1) == width - 1, 0.0, pltpu.roll(x, width - 1, 1))


def swap_blocks(arrays):
    arrays = list(arrays)
    lane = iota(arrays[0].shape, 1) // 16
    for step in (1, 2, 4):
        upper = (lane & step) != 0
        for low in range(8):
            if low & step:
                continue
            a, b = arrays[low], arrays[low | step]
            arrays[low] = jnp.where(upper, pltpu.roll(b, 16 * step, 1), a)
            arrays[low | step] = jnp.where(upper, b, pltpu.roll(a, 128 - 16 * step, 1))
    return arrays


def cell_of_lane(lane):
    return (lane // 32) * 32 + 2 * (lane % 16) + (lane // 16) % 2


def pack_kernel(image_ref, group_ref, cot_ref, send_ref):
    pick = jnp.where(cell_of_lane(iota((128, 128), 1)) == iota((128, 128), 0), 1.0, 0.0)
    pixels = tn(image_ref[...], pick.astype(BF16)).astype(BF16)
    taps = swap_blocks([group_ref[t].astype(F32) for t in range(8)])
    last = [group_ref[8, 16 * b : 16 * b + 16, :].astype(F32) for b in range(5)]
    last = swap_blocks(last + [jnp.zeros((16, 128), F32)] * 3)
    for p in range(8):
        send_ref[p, 0:80, :] = pixels[80 * p : 80 * p + 80]
        send_ref[p, 80:160, :] = taps[p].astype(BF16)
        send_ref[p, 160:176, :] = last[p].astype(BF16)
        for k in range(5):
            send_ref[p, 176 + 32 * k : 208 + 32 * k, :] = cot_ref[:, 128 * k : 128 * k + 128]


def spread_kernel(
    recv_ref, above_ref, below_ref,
    win_ref, down_ref, up_ref, own_ref, cot_ref, halo_ref, cell_ref, tap_ref,
):
    pixels = swap_blocks([recv_ref[q, 0:80, :].astype(F32) for q in range(8)])
    for r in range(4):
        columns = (from_left(pixels[2 * r + 1]), pixels[2 * r], pixels[2 * r + 1])
        for b in range(3):
            part = columns[b].astype(BF16)
            for i in range(2):
                a = r + 1 - 2 * i
                if 0 <= a < 3:
                    t = 3 * a + b
                    win_ref[80 * t : 80 * t + 80, 128 * i : 128 * i + 128] = part
    win_ref[0:240, 0:128] = jnp.zeros((240, 128), BF16)
    down_ref[:, 0:128] = pixels[6].astype(BF16)
    down_ref[:, 128:256] = pixels[7].astype(BF16)
    for q in range(8):
        tap_ref[80 * q : 80 * q + 80, 0:128] = recv_ref[q, 80:160, :]
        last = recv_ref[q, 160:176, :].astype(F32)
        for b in range(5):
            moved = last if b == 0 else pltpu.roll(last, 128 - 16 * b, 1)
            tap_ref[80 * q + 16 * b : 80 * q + 16 * b + 16, 128:256] = moved.astype(BF16)
        for k in range(5):
            for i in range(2):
                start = 176 + 32 * k + 16 * i
                cell_ref[128 * i + 16 * q : 128 * i + 16 * q + 16, 128 * k : 128 * k + 128] = recv_ref[q, start : start + 16, :]
    eye = jnp.where(iota((128, 128), 0) == iota((128, 128), 1), 1.0, 0.0).astype(BF16)
    for g in range(5):
        rows = slice(128 * g, 128 * g + 128)
        cot = nt(eye, cell_ref[:, rows]).astype(BF16)
        cot_ref[rows, :] = cot
        terms = tn(tap_ref[rows, :], cot)
        sums = []
        for u in range(3):
            base = 48 * u
            by_row = []
            for i in range(2):
                lanes = slice(128 * i, 128 * i + 128)
                by_row.append(
                    from_right(terms[base : base + 16, lanes])
                    + terms[base + 16 : base + 32, lanes]
                    + from_left(terms[base + 32 : base + 48, lanes])
                )
            sums.append(by_row)
        here = slice(16 * g, 16 * g + 16)
        own_ref[here, 0:128] = sums[1][0] + sums[0][1]
        own_ref[here, 128:256] = sums[1][1] + sums[2][0]
        up_ref[here, :] = sums[0][0]
        down_ref[here, 256:384] = sums[2][1].astype(BF16)
        halo_ref[here, 0:128] = above_ref[:, rows]
        halo_ref[here, 128:256] = below_ref[:, rows]


def forward_kernel(part_ref, down_ref, up_ref, weight_ref, hid_ref, win_ref, pass_ref):
    even = down_ref[:, 0:128]
    odd = down_ref[:, 128:256]
    win_ref[...] = part_ref[...]
    win_ref[0:80, 0:128] = from_left(odd.astype(F32)).astype(BF16)
    win_ref[80:160, 0:128] = even
    win_ref[160:240, 0:128] = odd
    pass_ref[...] = up_ref[...]
    hidden = tn(weight_ref[...], win_ref[...]).astype(BF16)
    for p in range(8):
        for g in range(5):
            hid_ref[p, 16 * g : 16 * g + 16, :] = hidden[128 * g + 16 * p : 128 * g + 16 * p + 16]


def middle_kernel(hid_ref, own_ref, down_ref, up_ref, halo_ref, act_ref, share_ref):
    hidden = hid_ref[0].astype(F32)
    for q in range(1, 8):
        hidden = hidden + hid_ref[q].astype(F32)
    cumul = 0.5 * (1.0 + lax.erf(hidden * (1.0 / math.sqrt(2.0))))
    density = jnp.exp(-0.5 * hidden * hidden) * (1.0 / math.sqrt(2.0 * math.pi))
    act_ref[...] = (hidden * cumul).astype(BF16)
    slopes = cumul + hidden * density
    act_grad = own_ref[...] + jnp.concatenate([down_ref[:, 256:384].astype(F32), up_ref[...]], axis=1)
    share_ref[0:80, :] = (act_grad * slopes).astype(BF16)
    share_ref[80:160, :] = halo_ref[...]


def backward_kernel(
    all_ref, weight_ref, win_ref, cot_ref, act_ref,
    img_ref, up_ref, red_ref, pre_ref, shift_ref, cell_ref,
):
    for p in range(8):
        for g in range(5):
            pre_ref[128 * g + 16 * p : 128 * g + 16 * p + 16, :] = all_ref[p, 16 * g : 16 * g + 16, :]
    pre = pre_ref[...]
    back = nn(weight_ref[...], pre)

    def term(a, b, i):
        t = 3 * a + b
        return back[80 * t : 80 * t + 80, 128 * i : 128 * i + 128]

    for i in range(2):
        img_ref[4 * i] = term(1, 1, i)
        img_ref[4 * i + 1] = term(1, 2, i) + from_right(term(1, 0, i))
    upper_even = [term(0, 1, i) for i in range(2)]
    upper_odd = [term(0, 2, i) + from_right(term(0, 0, i)) for i in range(2)]
    lower_odd = [term(2, 2, i) + from_right(term(2, 0, i)) for i in range(2)]
    img_ref[2] = term(2, 1, 0) + upper_even[1]
    img_ref[3] = lower_odd[0] + upper_odd[1]
    img_ref[6] = term(2, 1, 1)
    img_ref[7] = lower_odd[1]
    up_ref[0] = upper_even[0]
    up_ref[1] = upper_odd[0]

    red_ref[:, 0:640] = nt(pre, win_ref[0:640, :]).astype(BF16)
    rows = [act_ref[:, 128 * i : 128 * i + 128].astype(F32) for i in range(2)]
    moved = [[move(x).astype(BF16) for x in rows] for move in (from_left, lambda x: x, from_right)]
    shift_ref[...] = jnp.zeros((5, 256, 512), BF16)
    for g in range(5):
        for u in range(3):
            for v in range(3):
                base = 80 + 16 * (3 * u + v)
                for i in range(2):
                    lanes = slice(128 * (i + 2 - u), 128 * (i + 2 - u) + 128)
                    shift_ref[g, base : base + 16, lanes] = moved[v][i][16 * g : 16 * g + 16]
    for q in range(8):
        for k in range(5):
            for side in range(2):
                cell_ref[128 * side + 16 * q : 128 * side + 16 * q + 16, 128 * k : 128 * k + 128] = all_ref[
                    q, 80 + 16 * k : 96 + 16 * k, 128 * side : 128 * side + 128
                ]
    eye = jnp.where(iota((128, 128), 0) == iota((128, 128), 1), 1.0, 0.0).astype(BF16)
    tail = jnp.concatenate([win_ref[640:720, :], jnp.zeros((176, 256), BF16)], axis=0)
    last = nt(pre, tail)
    for g in range(5):
        here = slice(128 * g, 128 * g + 128)
        rims = nt(eye, cell_ref[:, here]).astype(BF16)
        cot = jnp.concatenate([rims[:, 0:128], cot_ref[here, :], rims[:, 128:256]], axis=1)
        red_ref[here, 640:896] = (last[here] + nt(cot, shift_ref[g])).astype(BF16)


def return_kernel(img_ref, below_ref, send_ref):
    parts = [img_ref[k] for k in range(8)]
    parts[6] = parts[6] + below_ref[0]
    parts[7] = parts[7] + below_ref[1]
    for q, x in enumerate(swap_blocks(parts)):
        send_ref[q] = x.astype(BF16)


def fold_kernel(high_ref, red_ref, keep_ref, give_ref):
    total = red_ref[0].astype(F32)
    for q in range(1, 16):
        total = total + red_ref[q].astype(F32)
    first, second = total[0:20], total[20:40]
    high = high_ref[0] == 1
    keep_ref[...] = jnp.where(high, second, first)
    give_ref[...] = jnp.where(high, first, second)


def unpack_kernel(recv_ref, out_ref):
    lane = iota((128, 128), 1)
    pick = jnp.where(cell_of_lane(lane) == iota((128, 128), 0), 1.0, 0.0).astype(BF16)
    for p in range(5):
        out_ref[:, 128 * p : 128 * p + 128] = nt(pick, recv_ref[128 * p : 128 * p + 128, :]).astype(BF16)


def finish_kernel(keep_ref, given_ref, conv_ref, group_ref):
    total = keep_ref[...] + given_ref[...]
    for t in range(9):
        conv_ref[t] = total[:, 80 * t : 80 * t + 80]
    group_ref[...] = jnp.transpose(total[:, 640:896])[80:224]


def call(kernel, outs, *args, scratch=(), smem=0):
    whole = [pl.BlockSpec(memory_space=pltpu.SMEM)] * smem
    whole += [pl.BlockSpec(memory_space=pltpu.VMEM)] * (len(args) - smem)
    return pl.pallas_call(
        kernel,
        out_shape=[jax.ShapeDtypeStruct(shape, dtype) for shape, dtype in outs],
        in_specs=whole,
        out_specs=[pl.BlockSpec(memory_space=pltpu.VMEM)] * len(outs),
        scratch_shapes=list(scratch),
        compiler_params=PARAMS,
    )(*args)


def per_device(image, conv_weight, group_weight, cotangent):
    tiles = lax.axis_size("tile")
    downward = [(i, i + 1) for i in range(tiles - 1)]
    upward = [(i + 1, i) for i in range(tiles - 1)]
    partners = [(i, i ^ 1) for i in range(tiles)]
    planes = [[2 * i + z for i in range(tiles // 2)] for z in range(2)]

    cells = cotangent.reshape(32, 640)
    above = lax.ppermute(cotangent[1], "tile", downward)
    below = lax.ppermute(cotangent[0], "tile", upward)
    weights = conv_weight.transpose(1, 0, 2).reshape(720, 640)
    (send,) = call(
        pack_kernel, [((8, 336, 128), BF16)],
        image.reshape(128, 640), group_weight.transpose(0, 2, 1), cells,
    )
    recv = lax.all_to_all(send, "fsdp", 0, 0, tiled=True)
    windows, down, up, own, cot, halo = call(
        spread_kernel,
        [((720, 256), BF16), ((80, 384), BF16), ((80, 128), F32), ((80, 256), F32), ((640, 256), BF16), ((80, 256), BF16)],
        recv, above, below,
        scratch=[pltpu.VMEM((256, 640), BF16), pltpu.VMEM((640, 256), BF16)],
    )
    down = lax.ppermute(down, "tile", downward)
    hid, windows, up = call(
        forward_kernel,
        [((8, 80, 256), BF16), ((720, 256), BF16), ((80, 128), F32)],
        windows, down, up, weights,
    )
    up = lax.ppermute(up, "tile", upward)
    hid = lax.all_to_all(hid, "fsdp", 0, 0, tiled=True)
    act, share = call(
        middle_kernel, [((80, 256), BF16), ((160, 256), BF16)], hid, own, down, up, halo
    )
    share_all = lax.all_gather(share, "fsdp", axis=0, tiled=False)
    img, img_up, red = call(
        backward_kernel,
        [((8, 80, 128), F32), ((2, 80, 128), F32), ((640, 896), BF16)],
        share_all, weights, windows, cot, act,
        scratch=[pltpu.VMEM((640, 256), BF16), pltpu.VMEM((5, 256, 512), BF16), pltpu.VMEM((256, 640), BF16)],
    )
    img_below = lax.ppermute(img_up, "tile", upward)
    red = lax.all_to_all(
        red.reshape(16, 40, 896), "tile", 0, 0, tiled=True, axis_index_groups=planes
    )
    (back,) = call(return_kernel, [((8, 80, 128), BF16)], img, img_below)
    back = lax.all_to_all(back, "fsdp", 0, 0, tiled=True)
    high = (lax.axis_index("tile") % 2).astype(jnp.int32).reshape(1)
    keep, give = call(fold_kernel, [((20, 896), F32), ((20, 896), F32)], high, red, smem=1)
    given = lax.ppermute(give, "tile", partners)
    (image_grad,) = call(unpack_kernel, [((128, 640), BF16)], back.reshape(640, 128))
    conv_weight_grad, group_weight_grad = call(
        finish_kernel, [((9, 20, 80), F32), ((144, 20), F32)], keep, given
    )
    conv_weight_grad = conv_weight_grad.transpose(2, 0, 1)
    group_weight_grad = group_weight_grad.reshape(9, 16, 20)
    return (image_grad.reshape(4, 32, 640), conv_weight_grad, group_weight_grad)


def solution(mesh):
    placed = (
        P("tile", "fsdp", None),
        P("fsdp", None, None),
        P(None, None, "fsdp"),
        P("tile", "fsdp", None),
    )
    return jax.shard_map(
        per_device,
        mesh=mesh,
        in_specs=placed,
        out_specs=(P("tile", "fsdp", None), P("fsdp", None, "tile"), P(None, "fsdp", "tile")),
        check_vma=False,
    )
```

```python
import functools
import math

import jax
import jax.numpy as jnp
from jax import lax
from jax.experimental import pallas as pl
from jax.experimental.pallas import tpu as pltpu
from jax.sharding import PartitionSpec as P

F32 = jnp.float32
BF16 = jnp.bfloat16
USUAL = 48 * 1024 * 1024
LARGE = 64 * 1024 * 1024 - 256 * 1024


def nn(a, b):
    return lax.dot_general(a, b, (((1,), (0,)), ((), ())), preferred_element_type=F32)


def nt(a, b):
    return lax.dot_general(a, b, (((1,), (1,)), ((), ())), preferred_element_type=F32)


def tn(a, b):
    return lax.dot_general(a, b, (((0,), (0,)), ((), ())), preferred_element_type=F32)


def iota(shape, dim):
    return lax.broadcasted_iota(jnp.int32, shape, dim)


def from_left(x):
    return jnp.where(iota(x.shape, 1) == 0, 0.0, pltpu.roll(x, 1, 1))


def from_right(x):
    width = x.shape[1]
    return jnp.where(iota(x.shape, 1) == width - 1, 0.0, pltpu.roll(x, width - 1, 1))


def swap_blocks(arrays):
    arrays = list(arrays)
    lane = iota(arrays[0].shape, 1) // 16
    for step in (1, 2, 4):
        upper = (lane & step) != 0
        for low in range(8):
            if low & step:
                continue
            a, b = arrays[low], arrays[low | step]
            arrays[low] = jnp.where(upper, pltpu.roll(b, 16 * step, 1), a)
            arrays[low | step] = jnp.where(upper, b, pltpu.roll(a, 128 - 16 * step, 1))
    return arrays


def cell_of_lane(lane):
    return (lane // 32) * 32 + 2 * (lane % 16) + (lane // 16) % 2


def pack_kernel(image_hbm, group_hbm, cot_hbm, send_ref, image_ref, group_ref, cot_ref, sems):
    copies = [
        pltpu.make_async_copy(group_hbm, group_ref, sems.at[0]),
        pltpu.make_async_copy(image_hbm, image_ref, sems.at[1]),
        pltpu.make_async_copy(cot_hbm, cot_ref, sems.at[2]),
    ]
    for copy in copies:
        copy.start()
    for copy in copies:
        copy.wait()
    pick = jnp.where(cell_of_lane(iota((128, 128), 1)) == iota((128, 128), 0), 1.0, 0.0)
    pixels = tn(image_ref[...], pick.astype(BF16)).astype(BF16)
    taps = swap_blocks([group_ref[t].astype(F32) for t in range(8)])
    last = [group_ref[8, 16 * b : 16 * b + 16, :].astype(F32) for b in range(5)]
    last = swap_blocks(last + [jnp.zeros((16, 128), F32)] * 3)
    for p in range(8):
        send_ref[p, 0:80, :] = pixels[80 * p : 80 * p + 80]
        send_ref[p, 80:160, :] = taps[p].astype(BF16)
        send_ref[p, 160:176, :] = last[p].astype(BF16)
        for k in range(5):
            send_ref[p, 176 + 32 * k : 208 + 32 * k, :] = cot_ref[:, 128 * k : 128 * k + 128]


def spread_kernel(
    recv_ref, raw_ref, win_ref, down_ref, up_ref, own_ref, cot_ref, cell_ref, tap_ref
):
    pixels = swap_blocks([recv_ref[q, 0:80, :].astype(F32) for q in range(8)])
    for r in range(4):
        columns = (from_left(pixels[2 * r + 1]), pixels[2 * r], pixels[2 * r + 1])
        for b in range(3):
            part = columns[b].astype(BF16)
            for i in range(2):
                a = r + 1 - 2 * i
                if 0 <= a < 3:
                    t = 3 * a + b
                    win_ref[80 * t : 80 * t + 80, 128 * i : 128 * i + 128] = part
    win_ref[0:240, 0:128] = jnp.zeros((240, 128), BF16)
    down_ref[:, 0:128] = pixels[6].astype(BF16)
    down_ref[:, 128:256] = pixels[7].astype(BF16)
    for q in range(8):
        tap_ref[80 * q : 80 * q + 80, 0:128] = recv_ref[q, 80:160, :]
        last = recv_ref[q, 160:176, :].astype(F32)
        for b in range(5):
            moved = last if b == 0 else pltpu.roll(last, 128 - 16 * b, 1)
            tap_ref[80 * q + 16 * b : 80 * q + 16 * b + 16, 128:256] = moved.astype(BF16)
        for k in range(5):
            for i in range(2):
                start = 176 + 32 * k + 16 * i
                cell_ref[128 * i + 16 * q : 128 * i + 16 * q + 16, 128 * k : 128 * k + 128] = recv_ref[q, start : start + 16, :]
    eye = jnp.where(iota((128, 128), 0) == iota((128, 128), 1), 1.0, 0.0).astype(BF16)
    for g in range(5):
        rows = slice(128 * g, 128 * g + 128)
        cot = nt(eye, cell_ref[:, rows]).astype(BF16)
        cot_ref[rows, :] = cot
        terms = tn(tap_ref[rows, :], cot)
        sums = []
        for u in range(3):
            base = 48 * u
            by_row = []
            for i in range(2):
                lanes = slice(128 * i, 128 * i + 128)
                by_row.append(
                    from_right(terms[base : base + 16, lanes])
                    + terms[base + 16 : base + 32, lanes]
                    + from_left(terms[base + 32 : base + 48, lanes])
                )
            sums.append(by_row)
        here = slice(16 * g, 16 * g + 16)
        own_ref[here, 0:128] = sums[1][0] + sums[0][1]
        own_ref[here, 128:256] = sums[1][1] + sums[2][0]
        up_ref[here, 0:128] = sums[0][0].astype(BF16)
        up_ref[here, 128:256] = raw_ref[0:16, rows]
        down_ref[here, 256:384] = sums[2][1].astype(BF16)
        down_ref[here, 384:512] = raw_ref[16:32, rows]


def forward_kernel(part_ref, down_ref, up_ref, weight_ref, hid_ref, win_ref, pass_ref):
    even = down_ref[:, 0:128]
    odd = down_ref[:, 128:256]
    win_ref[...] = part_ref[...]
    win_ref[0:80, 0:128] = from_left(odd.astype(F32)).astype(BF16)
    win_ref[80:160, 0:128] = even
    win_ref[160:240, 0:128] = odd
    pass_ref[...] = up_ref[...]
    hidden = tn(weight_ref[...], win_ref[...]).astype(BF16)
    for p in range(8):
        for g in range(5):
            hid_ref[p, 16 * g : 16 * g + 16, :] = hidden[128 * g + 16 * p : 128 * g + 16 * p + 16]


def middle_kernel(hid_ref, own_ref, down_ref, up_ref, act_ref, share_ref):
    hidden = hid_ref[0].astype(F32)
    for q in range(1, 8):
        hidden = hidden + hid_ref[q].astype(F32)
    cumul = 0.5 * (1.0 + lax.erf(hidden * (1.0 / math.sqrt(2.0))))
    density = jnp.exp(-0.5 * hidden * hidden) * (1.0 / math.sqrt(2.0 * math.pi))
    act_ref[...] = (hidden * cumul).astype(BF16)
    slopes = cumul + hidden * density
    act_grad = own_ref[...] + jnp.concatenate(
        [down_ref[:, 256:384].astype(F32), up_ref[:, 0:128].astype(F32)], axis=1
    )
    share_ref[0:80, :] = (act_grad * slopes).astype(BF16)
    share_ref[80:160, 0:128] = down_ref[:, 384:512]
    share_ref[80:160, 128:256] = up_ref[:, 128:256]


def weight_grad_kernel(all_ref, win_ref, cot_ref, act_ref, red_ref, pre_ref, shift_ref, cell_ref):
    for p in range(8):
        for g in range(5):
            pre_ref[128 * g + 16 * p : 128 * g + 16 * p + 16, :] = all_ref[p, 16 * g : 16 * g + 16, :]
    pre = pre_ref[...]
    red_ref[:, 0:640] = nt(pre, win_ref[0:640, :]).astype(BF16)
    rows = [act_ref[:, 128 * i : 128 * i + 128].astype(F32) for i in range(2)]
    moved = [[move(x).astype(BF16) for x in rows] for move in (from_left, lambda x: x, from_right)]
    shift_ref[...] = jnp.zeros((5, 256, 512), BF16)
    for g in range(5):
        for u in range(3):
            for v in range(3):
                base = 80 + 16 * (3 * u + v)
                for i in range(2):
                    lanes = slice(128 * (i + 2 - u), 128 * (i + 2 - u) + 128)
                    shift_ref[g, base : base + 16, lanes] = moved[v][i][16 * g : 16 * g + 16]
    for q in range(8):
        for k in range(5):
            for side in range(2):
                cell_ref[128 * side + 16 * q : 128 * side + 16 * q + 16, 128 * k : 128 * k + 128] = all_ref[
                    q, 80 + 16 * k : 96 + 16 * k, 128 * side : 128 * side + 128
                ]
    eye = jnp.where(iota((128, 128), 0) == iota((128, 128), 1), 1.0, 0.0).astype(BF16)
    tail = jnp.concatenate([win_ref[640:720, :], jnp.zeros((176, 256), BF16)], axis=0)
    last = nt(pre, tail)
    for g in range(5):
        here = slice(128 * g, 128 * g + 128)
        rims = nt(eye, cell_ref[:, here]).astype(BF16)
        cot = jnp.concatenate([rims[:, 0:128], cot_ref[here, :], rims[:, 128:256]], axis=1)
        red_ref[here, 640:896] = (last[here] + nt(cot, shift_ref[g])).astype(BF16)


def image_grad_kernel(pre_ref, weight_ref, img_ref, up_ref):
    pre = pre_ref[...]
    back = nn(weight_ref[...], pre)

    def term(a, b, i):
        t = 3 * a + b
        return back[80 * t : 80 * t + 80, 128 * i : 128 * i + 128]

    for i in range(2):
        img_ref[4 * i] = term(1, 1, i)
        img_ref[4 * i + 1] = term(1, 2, i) + from_right(term(1, 0, i))
    upper_even = [term(0, 1, i) for i in range(2)]
    upper_odd = [term(0, 2, i) + from_right(term(0, 0, i)) for i in range(2)]
    lower_odd = [term(2, 2, i) + from_right(term(2, 0, i)) for i in range(2)]
    img_ref[2] = term(2, 1, 0) + upper_even[1]
    img_ref[3] = lower_odd[0] + upper_odd[1]
    img_ref[6] = term(2, 1, 1)
    img_ref[7] = lower_odd[1]
    up_ref[0] = upper_even[0]
    up_ref[1] = upper_odd[0]


def return_kernel(img_ref, below_ref, send_ref):
    parts = [img_ref[k] for k in range(8)]
    parts[6] = parts[6] + below_ref[0]
    parts[7] = parts[7] + below_ref[1]
    for q, x in enumerate(swap_blocks(parts)):
        send_ref[q] = x.astype(BF16)


def fold_kernel(high_ref, red_ref, keep_ref, give_ref):
    total = red_ref[0].astype(F32)
    for q in range(1, 16):
        total = total + red_ref[q].astype(F32)
    first, second = total[0:20], total[20:40]
    high = high_ref[0] == 1
    keep_ref[...] = jnp.where(high, second, first)
    give_ref[...] = jnp.where(high, first, second).astype(BF16)


def unpack_kernel(recv_ref, out_ref):
    lane = iota((128, 128), 1)
    pick = jnp.where(cell_of_lane(lane) == iota((128, 128), 0), 1.0, 0.0).astype(BF16)
    for p in range(5):
        out_ref[:, 128 * p : 128 * p + 128] = nt(pick, recv_ref[128 * p : 128 * p + 128, :]).astype(BF16)


def finish_kernel(keep_ref, given_ref, conv_ref, group_ref):
    total = keep_ref[...] + given_ref[...].astype(F32)
    for t in range(9):
        conv_ref[t] = total[:, 80 * t : 80 * t + 80]
    group_ref[...] = jnp.transpose(total[:, 640:896])[80:224]


def call(kernel, outs, *args, scratch=(), smem=0, space=pltpu.VMEM, limit=USUAL):
    whole = [pl.BlockSpec(memory_space=pltpu.SMEM)] * smem
    whole += [pl.BlockSpec(memory_space=space)] * (len(args) - smem)
    return pl.pallas_call(
        kernel,
        out_shape=[jax.ShapeDtypeStruct(shape, dtype) for shape, dtype in outs],
        in_specs=whole,
        out_specs=[pl.BlockSpec(memory_space=pltpu.VMEM)] * len(outs),
        scratch_shapes=list(scratch),
        compiler_params=pltpu.CompilerParams(vmem_limit_bytes=limit),
    )(*args)


def per_device(image, conv_weight, group_weight, cotangent):
    tiles = lax.axis_size("tile")
    downward = [(i, i + 1) for i in range(tiles - 1)]
    upward = [(i + 1, i) for i in range(tiles - 1)]
    partners = [(i, i ^ 1) for i in range(tiles)]
    planes = [[2 * i + z for i in range(tiles // 2)] for z in range(2)]

    cells = cotangent.reshape(32, 640)
    weights = conv_weight.transpose(1, 0, 2).reshape(720, 640)
    (send,) = call(
        pack_kernel, [((8, 336, 128), BF16)],
        image.reshape(128, 640), group_weight.transpose(0, 2, 1), cells,
        scratch=[pltpu.VMEM((128, 640), BF16), pltpu.VMEM((9, 80, 128), BF16), pltpu.VMEM((32, 640), BF16), pltpu.SemaphoreType.DMA((3,))],
        space=pl.ANY,
        limit=LARGE,
    )
    recv = lax.all_to_all(send, "fsdp", 0, 0, tiled=True)
    windows, down, up, own, cot = call(
        spread_kernel,
        [((720, 256), BF16), ((80, 512), BF16), ((80, 256), BF16), ((80, 256), F32), ((640, 256), BF16)],
        recv, cells,
        scratch=[pltpu.VMEM((256, 640), BF16), pltpu.VMEM((640, 256), BF16)],
    )
    down = lax.ppermute(down, "tile", downward)
    hid, windows, up = call(
        forward_kernel,
        [((8, 80, 256), BF16), ((720, 256), BF16), ((80, 256), BF16)],
        windows, down, up, weights,
    )
    up = lax.ppermute(up, "tile", upward)
    hid = lax.all_to_all(hid, "fsdp", 0, 0, tiled=True)
    act, share = call(
        middle_kernel, [((80, 256), BF16), ((160, 256), BF16)], hid, own, down, up
    )
    share_all = lax.all_gather(share, "fsdp", axis=0, tiled=False)
    red, pre = call(
        weight_grad_kernel,
        [((640, 896), BF16), ((640, 256), BF16)],
        share_all, windows, cot, act,
        scratch=[pltpu.VMEM((5, 256, 512), BF16), pltpu.VMEM((256, 640), BF16)],
    )
    img, img_up = call(
        image_grad_kernel, [((8, 80, 128), F32), ((2, 80, 128), F32)], pre, weights
    )
    img_below = lax.ppermute(img_up, "tile", upward)
    red = lax.all_to_all(
        red.reshape(16, 40, 896), "tile", 0, 0, tiled=True, axis_index_groups=planes
    )
    (back,) = call(return_kernel, [((8, 80, 128), BF16)], img, img_below)
    back = lax.all_to_all(back, "fsdp", 0, 0, tiled=True)
    high = (lax.axis_index("tile") % 2).astype(jnp.int32).reshape(1)
    keep, give = call(fold_kernel, [((20, 896), F32), ((20, 896), BF16)], high, red, smem=1)
    given = lax.ppermute(give, "tile", partners)
    (image_grad,) = call(unpack_kernel, [((128, 640), BF16)], back.reshape(640, 128))
    conv_weight_grad, group_weight_grad = call(
        finish_kernel, [((9, 20, 80), F32), ((144, 20), F32)], keep, given
    )
    conv_weight_grad = conv_weight_grad.transpose(2, 0, 1)
    group_weight_grad = group_weight_grad.reshape(9, 16, 20)
    return (image_grad.reshape(4, 32, 640), conv_weight_grad, group_weight_grad)


def solution(mesh):
    placed = (
        P("tile", "fsdp", None),
        P("fsdp", None, None),
        P(None, None, "fsdp"),
        P("tile", "fsdp", None),
    )
    return jax.shard_map(
        per_device,
        mesh=mesh,
        in_specs=placed,
        out_specs=(P("tile", "fsdp", None), P("fsdp", None, "tile"), P(None, "fsdp", "tile")),
        check_vma=False,
    )
```

```python
import functools
import math

import jax
import jax.numpy as jnp
from jax import lax
from jax.experimental import pallas as pl
from jax.experimental.pallas import tpu as pltpu
from jax.sharding import PartitionSpec as P

F32 = jnp.float32
BF16 = jnp.bfloat16
FORWARD_FLOPS = 12_000_000_000


def nn(a, b):
    return lax.dot_general(a, b, (((1,), (0,)), ((), ())), preferred_element_type=F32)


def nt(a, b):
    return lax.dot_general(a, b, (((1,), (1,)), ((), ())), preferred_element_type=F32)


def tn(a, b):
    return lax.dot_general(a, b, (((0,), (0,)), ((), ())), preferred_element_type=F32)


def iota(shape, dim):
    return lax.broadcasted_iota(jnp.int32, shape, dim)


def from_left(x):
    return jnp.where(iota(x.shape, 1) == 0, 0.0, pltpu.roll(x, 1, 1))


def from_right(x):
    width = x.shape[1]
    return jnp.where(iota(x.shape, 1) == width - 1, 0.0, pltpu.roll(x, width - 1, 1))


def swap_blocks(arrays):
    arrays = list(arrays)
    lane = iota(arrays[0].shape, 1) // 16
    for step in (1, 2, 4):
        upper = (lane & step) != 0
        for low in range(8):
            if low & step:
                continue
            a, b = arrays[low], arrays[low | step]
            arrays[low] = jnp.where(upper, pltpu.roll(b, 16 * step, 1), a)
            arrays[low | step] = jnp.where(upper, b, pltpu.roll(a, 128 - 16 * step, 1))
    return arrays


def cell_of_lane(lane):
    return (lane // 32) * 32 + 2 * (lane % 16) + (lane // 16) % 2


def pack_kernel(slot_ref, image_ref, group_ref, cot_ref, *refs):
    *send_refs, block_ref = refs
    pick = jnp.where(cell_of_lane(iota((128, 128), 1)) == iota((128, 128), 0), 1.0, 0.0)
    pixels = tn(image_ref[...], pick.astype(BF16)).astype(BF16)
    taps = swap_blocks([group_ref[t].astype(F32) for t in range(8)])
    last = [group_ref[8, 16 * b : 16 * b + 16, :].astype(F32) for b in range(5)]
    last = swap_blocks(last + [jnp.zeros((16, 128), F32)] * 3)
    for p in range(8):
        block_ref[p, 0:80, :] = pixels[80 * p : 80 * p + 80]
        block_ref[p, 80:160, :] = taps[p].astype(BF16)
        block_ref[p, 160:176, :] = last[p].astype(BF16)
    for k in range(8):
        send_refs[k][0:176, :] = block_ref[slot_ref[0] ^ k]
        for j in range(5):
            send_refs[k][176 + 32 * j : 208 + 32 * j, :] = cot_ref[:, 128 * j : 128 * j + 128]


def spread_kernel(slot_ref, raw_ref, *refs):
    *recv_refs, win_ref, down_ref, up_ref, own_ref, cot_ref, cell_ref, tap_ref, block_ref = refs
    for k in range(8):
        block_ref[slot_ref[0] ^ k] = recv_refs[k][...]
    pixels = swap_blocks([block_ref[q, 0:80, :].astype(F32) for q in range(8)])
    for r in range(4):
        columns = (from_left(pixels[2 * r + 1]), pixels[2 * r], pixels[2 * r + 1])
        for b in range(3):
            part = columns[b].astype(BF16)
            for i in range(2):
                a = r + 1 - 2 * i
                if 0 <= a < 3:
                    t = 3 * a + b
                    win_ref[80 * t : 80 * t + 80, 128 * i : 128 * i + 128] = part
    win_ref[0:240, 0:128] = jnp.zeros((240, 128), BF16)
    down_ref[:, 0:128] = pixels[6].astype(BF16)
    down_ref[:, 128:256] = pixels[7].astype(BF16)
    for q in range(8):
        tap_ref[80 * q : 80 * q + 80, 0:128] = block_ref[q, 80:160, :]
        last = block_ref[q, 160:176, :].astype(F32)
        for b in range(5):
            moved = last if b == 0 else pltpu.roll(last, 128 - 16 * b, 1)
            tap_ref[80 * q + 16 * b : 80 * q + 16 * b + 16, 128:256] = moved.astype(BF16)
        for k in range(5):
            for i in range(2):
                start = 176 + 32 * k + 16 * i
                cell_ref[128 * i + 16 * q : 128 * i + 16 * q + 16, 128 * k : 128 * k + 128] = block_ref[q, start : start + 16, :]
    eye = jnp.where(iota((128, 128), 0) == iota((128, 128), 1), 1.0, 0.0).astype(BF16)
    for g in range(5):
        rows = slice(128 * g, 128 * g + 128)
        cot = nt(eye, cell_ref[:, rows]).astype(BF16)
        cot_ref[rows, :] = cot
        terms = tn(tap_ref[rows, :], cot)
        sums = []
        for u in range(3):
            base = 48 * u
            by_row = []
            for i in range(2):
                lanes = slice(128 * i, 128 * i + 128)
                by_row.append(
                    from_right(terms[base : base + 16, lanes])
                    + terms[base + 16 : base + 32, lanes]
                    + from_left(terms[base + 32 : base + 48, lanes])
                )
            sums.append(by_row)
        here = slice(16 * g, 16 * g + 16)
        own_ref[here, 0:128] = sums[1][0] + sums[0][1]
        own_ref[here, 128:256] = sums[1][1] + sums[2][0]
        up_ref[here, 0:128] = sums[0][0].astype(BF16)
        up_ref[here, 128:256] = raw_ref[0:16, rows]
        down_ref[here, 256:384] = sums[2][1].astype(BF16)
        down_ref[here, 384:512] = raw_ref[16:32, rows]


def forward_kernel(slot_ref, part_ref, down_ref, weight_ref, *refs):
    *hid_refs, win_ref, block_ref = refs
    odd = down_ref[:, 128:256]
    win_ref[...] = part_ref[...]
    win_ref[0:80, 0:128] = from_left(odd.astype(F32)).astype(BF16)
    win_ref[80:160, 0:128] = down_ref[:, 0:128]
    win_ref[160:240, 0:128] = odd
    hidden = tn(weight_ref[...], win_ref[...]).astype(BF16)
    for p in range(8):
        for g in range(5):
            block_ref[p, 16 * g : 16 * g + 16, :] = hidden[128 * g + 16 * p : 128 * g + 16 * p + 16]
    for k in range(8):
        hid_refs[k][...] = block_ref[slot_ref[0] ^ k]


def middle_kernel(own_ref, down_ref, up_ref, *refs):
    *hid_refs, act_ref, share_ref = refs
    hidden = hid_refs[0][...].astype(F32)
    for k in range(1, 8):
        hidden = hidden + hid_refs[k][...].astype(F32)
    cumul = 0.5 * (1.0 + lax.erf(hidden * (1.0 / math.sqrt(2.0))))
    density = jnp.exp(-0.5 * hidden * hidden) * (1.0 / math.sqrt(2.0 * math.pi))
    act_ref[...] = (hidden * cumul).astype(BF16)
    slopes = cumul + hidden * density
    act_grad = own_ref[...] + jnp.concatenate(
        [down_ref[:, 256:384].astype(F32), up_ref[:, 0:128].astype(F32)], axis=1
    )
    share_ref[0:80, :] = (act_grad * slopes).astype(BF16)
    share_ref[80:160, 0:128] = down_ref[:, 384:512]
    share_ref[80:160, 128:256] = up_ref[:, 128:256]


def weight_grad_kernel(all_ref, win_ref, cot_ref, act_ref, red_ref, pre_ref, shift_ref, cell_ref):
    for p in range(8):
        for g in range(5):
            pre_ref[128 * g + 16 * p : 128 * g + 16 * p + 16, :] = all_ref[p, 16 * g : 16 * g + 16, :]
    pre = pre_ref[...]
    red_ref[:, 0:640] = nt(pre, win_ref[0:640, :]).astype(BF16)
    rows = [act_ref[:, 128 * i : 128 * i + 128].astype(F32) for i in range(2)]
    moved = [[move(x).astype(BF16) for x in rows] for move in (from_left, lambda x: x, from_right)]
    shift_ref[...] = jnp.zeros((5, 256, 512), BF16)
    for g in range(5):
        for u in range(3):
            for v in range(3):
                base = 80 + 16 * (3 * u + v)
                for i in range(2):
                    lanes = slice(128 * (i + 2 - u), 128 * (i + 2 - u) + 128)
                    shift_ref[g, base : base + 16, lanes] = moved[v][i][16 * g : 16 * g + 16]
    for q in range(8):
        for k in range(5):
            for side in range(2):
                cell_ref[128 * side + 16 * q : 128 * side + 16 * q + 16, 128 * k : 128 * k + 128] = all_ref[
                    q, 80 + 16 * k : 96 + 16 * k, 128 * side : 128 * side + 128
                ]
    eye = jnp.where(iota((128, 128), 0) == iota((128, 128), 1), 1.0, 0.0).astype(BF16)
    tail = jnp.concatenate([win_ref[640:720, :], jnp.zeros((176, 256), BF16)], axis=0)
    last = nt(pre, tail)
    for g in range(5):
        here = slice(128 * g, 128 * g + 128)
        rims = nt(eye, cell_ref[:, here]).astype(BF16)
        cot = jnp.concatenate([rims[:, 0:128], cot_ref[here, :], rims[:, 128:256]], axis=1)
        red_ref[here, 640:896] = (last[here] + nt(cot, shift_ref[g])).astype(BF16)


def image_grad_kernel(pre_ref, weight_ref, img_ref, up_ref):
    pre = pre_ref[...]
    back = nn(weight_ref[...], pre)

    def term(a, b, i):
        t = 3 * a + b
        return back[80 * t : 80 * t + 80, 128 * i : 128 * i + 128]

    for i in range(2):
        img_ref[4 * i] = term(1, 1, i)
        img_ref[4 * i + 1] = term(1, 2, i) + from_right(term(1, 0, i))
    upper_even = [term(0, 1, i) for i in range(2)]
    upper_odd = [term(0, 2, i) + from_right(term(0, 0, i)) for i in range(2)]
    lower_odd = [term(2, 2, i) + from_right(term(2, 0, i)) for i in range(2)]
    img_ref[2] = term(2, 1, 0) + upper_even[1]
    img_ref[3] = lower_odd[0] + upper_odd[1]
    img_ref[6] = term(2, 1, 1)
    img_ref[7] = lower_odd[1]
    up_ref[0] = upper_even[0]
    up_ref[1] = upper_odd[0]


def return_kernel(slot_ref, img_ref, below_ref, *refs):
    *send_refs, slot_blocks = refs
    parts = [img_ref[k] for k in range(8)]
    parts[6] = parts[6] + below_ref[0]
    parts[7] = parts[7] + below_ref[1]
    for q, x in enumerate(swap_blocks(parts)):
        slot_blocks[slot_ref[0] ^ q] = x.astype(BF16)
    for k in range(8):
        send_refs[k][...] = slot_blocks[k]


def fold_kernel(high_ref, red_ref, keep_ref, give_ref):
    total = red_ref[0].astype(F32)
    for q in range(1, 16):
        total = total + red_ref[q].astype(F32)
    first, second = total[0:20], total[20:40]
    high = high_ref[0] == 1
    keep_ref[...] = jnp.where(high, second, first)
    give_ref[...] = jnp.where(high, first, second).astype(BF16)


def unpack_kernel(slot_ref, *refs):
    *recv_refs, out_ref, block_ref = refs
    for k in range(8):
        block_ref[slot_ref[0] ^ k] = recv_refs[k][...]
    lane = iota((128, 128), 1)
    pick = jnp.where(cell_of_lane(lane) == iota((128, 128), 0), 1.0, 0.0).astype(BF16)
    blocks = block_ref[...].reshape(640, 128)
    for p in range(5):
        out_ref[:, 128 * p : 128 * p + 128] = nt(pick, blocks[128 * p : 128 * p + 128]).astype(BF16)


def finish_kernel(keep_ref, given_ref, conv_ref, group_ref):
    total = keep_ref[...] + given_ref[...].astype(F32)
    for t in range(9):
        conv_ref[t] = total[:, 80 * t : 80 * t + 80]
    group_ref[...] = jnp.transpose(total[:, 640:896])[80:224]


def call(kernel, outs, *args, scratch=(), smem=0, flops=0):
    whole = [pl.BlockSpec(memory_space=pltpu.SMEM)] * smem
    whole += [pl.BlockSpec(memory_space=pltpu.VMEM)] * (len(args) - smem)
    return pl.pallas_call(
        kernel,
        out_shape=[jax.ShapeDtypeStruct(shape, dtype) for shape, dtype in outs],
        in_specs=whole,
        out_specs=[pl.BlockSpec(memory_space=pltpu.VMEM)] * len(outs),
        scratch_shapes=list(scratch),
        compiler_params=pltpu.CompilerParams(vmem_limit_bytes=48 * 1024 * 1024),
        cost_estimate=pl.CostEstimate(flops=flops, bytes_accessed=0, transcendentals=0) if flops else None,
    )(*args)


def trade(blocks):
    devices = range(8)
    return [blocks[0]] + [
        lax.ppermute(blocks[k], "fsdp", [(i, i ^ k) for i in devices]) for k in devices[1:]
    ]


def per_device(image, conv_weight, group_weight, cotangent):
    tiles = lax.axis_size("tile")
    downward = [(i, i + 1) for i in range(tiles - 1)]
    upward = [(i + 1, i) for i in range(tiles - 1)]
    partners = [(i, i ^ 1) for i in range(tiles)]
    planes = [[2 * i + z for i in range(tiles // 2)] for z in range(2)]

    cells = cotangent.reshape(32, 640)
    slot = lax.axis_index("fsdp").astype(jnp.int32).reshape(1)
    weights = conv_weight.transpose(1, 0, 2).reshape(720, 640)
    parts = trade(
        call(
            pack_kernel, [((336, 128), BF16)] * 8,
            slot, image.reshape(128, 640), group_weight.transpose(0, 2, 1), cells,
            scratch=[pltpu.VMEM((8, 176, 128), BF16)], smem=1,
        )
    )
    windows, down, up, own, cot = call(
        spread_kernel,
        [((720, 256), BF16), ((80, 512), BF16), ((80, 256), BF16), ((80, 256), F32), ((640, 256), BF16)],
        slot, cells, *parts,
        scratch=[pltpu.VMEM((256, 640), BF16), pltpu.VMEM((640, 256), BF16), pltpu.VMEM((8, 336, 128), BF16)],
        smem=1,
    )
    down = lax.ppermute(down, "tile", downward)
    *hid, windows = call(
        forward_kernel, [((80, 256), BF16)] * 8 + [((720, 256), BF16)],
        slot, windows, down, weights,
        scratch=[pltpu.VMEM((8, 80, 256), BF16)], smem=1, flops=FORWARD_FLOPS,
    )
    hid = trade(hid)
    up = lax.ppermute(up, "tile", upward)
    act, share = call(
        middle_kernel, [((80, 256), BF16), ((160, 256), BF16)], own, down, up, *hid
    )
    share_all = lax.all_gather(share, "fsdp", axis=0, tiled=False)
    red, pre = call(
        weight_grad_kernel,
        [((640, 896), BF16), ((640, 256), BF16)],
        share_all, windows, cot, act,
        scratch=[pltpu.VMEM((5, 256, 512), BF16), pltpu.VMEM((256, 640), BF16)],
    )
    img, img_up = call(
        image_grad_kernel, [((8, 80, 128), F32), ((2, 80, 128), F32)], pre, weights
    )
    img_below = lax.ppermute(img_up, "tile", upward)
    red = lax.all_to_all(
        red.reshape(16, 40, 896), "tile", 0, 0, tiled=True, axis_index_groups=planes
    )
    back = trade(
        call(
            return_kernel, [((80, 128), BF16)] * 8, slot, img, img_below,
            scratch=[pltpu.VMEM((8, 80, 128), BF16)], smem=1,
        )
    )
    high = (lax.axis_index("tile") % 2).astype(jnp.int32).reshape(1)
    keep, give = call(fold_kernel, [((20, 896), F32), ((20, 896), BF16)], high, red, smem=1)
    given = lax.ppermute(give, "tile", partners)
    (image_grad,) = call(
        unpack_kernel, [((128, 640), BF16)], slot, *back,
        scratch=[pltpu.VMEM((8, 80, 128), BF16)], smem=1,
    )
    conv_weight_grad, group_weight_grad = call(
        finish_kernel, [((9, 20, 80), F32), ((144, 20), F32)], keep, given
    )
    conv_weight_grad = conv_weight_grad.transpose(2, 0, 1)
    group_weight_grad = group_weight_grad.reshape(9, 16, 20)
    return (image_grad.reshape(4, 32, 640), conv_weight_grad, group_weight_grad)


def solution(mesh):
    placed = (
        P("tile", "fsdp", None),
        P("fsdp", None, None),
        P(None, None, "fsdp"),
        P("tile", "fsdp", None),
    )
    return jax.shard_map(
        per_device,
        mesh=mesh,
        in_specs=placed,
        out_specs=(P("tile", "fsdp", None), P("fsdp", None, "tile"), P(None, "fsdp", "tile")),
        check_vma=False,
    )
```

```python
import functools
import math

import jax
import jax.numpy as jnp
from jax import lax
from jax.experimental import pallas as pl
from jax.experimental.pallas import tpu as pltpu
from jax.sharding import PartitionSpec as P

F32 = jnp.float32
BF16 = jnp.bfloat16
ORDER = (0, 6, 7, 4, 5, 2, 3, 1)
FORWARD_FLOPS = 12_000_000_000


def nn(a, b):
    return lax.dot_general(a, b, (((1,), (0,)), ((), ())), preferred_element_type=F32)


def nt(a, b):
    return lax.dot_general(a, b, (((1,), (1,)), ((), ())), preferred_element_type=F32)


def tn(a, b):
    return lax.dot_general(a, b, (((0,), (0,)), ((), ())), preferred_element_type=F32)


def iota(shape, dim):
    return lax.broadcasted_iota(jnp.int32, shape, dim)


def from_left(x):
    return jnp.where(iota(x.shape, 1) == 0, 0.0, pltpu.roll(x, 1, 1))


def from_right(x):
    width = x.shape[1]
    return jnp.where(iota(x.shape, 1) == width - 1, 0.0, pltpu.roll(x, width - 1, 1))


def swap_blocks(arrays):
    arrays = list(arrays)
    lane = iota(arrays[0].shape, 1) // 16
    for step in (1, 2, 4):
        upper = (lane & step) != 0
        for low in range(8):
            if low & step:
                continue
            a, b = arrays[low], arrays[low | step]
            arrays[low] = jnp.where(upper, pltpu.roll(b, 16 * step, 1), a)
            arrays[low | step] = jnp.where(upper, b, pltpu.roll(a, 128 - 16 * step, 1))
    return arrays


def cell_of_lane(lane):
    return (lane // 32) * 32 + 2 * (lane % 16) + (lane // 16) % 2


def pack_kernel(slot_ref, image_ref, group_ref, cot_ref, *refs):
    *send_refs, block_ref = refs
    pick = jnp.where(cell_of_lane(iota((128, 128), 1)) == iota((128, 128), 0), 1.0, 0.0)
    pixels = tn(image_ref[...], pick.astype(BF16)).astype(BF16)
    taps = swap_blocks([group_ref[t].astype(F32) for t in range(8)])
    last = [group_ref[8, 16 * b : 16 * b + 16, :].astype(F32) for b in range(5)]
    last = swap_blocks(last + [jnp.zeros((16, 128), F32)] * 3)
    for p in range(8):
        block_ref[p, 0:80, :] = pixels[80 * p : 80 * p + 80]
        block_ref[p, 80:160, :] = taps[p].astype(BF16)
        block_ref[p, 160:176, :] = last[p].astype(BF16)
    for n, k in enumerate(ORDER):
        send_refs[n][0:176, :] = block_ref[slot_ref[0] ^ k]
        for j in range(5):
            send_refs[n][176 + 32 * j : 208 + 32 * j, :] = cot_ref[:, 128 * j : 128 * j + 128]


def spread_kernel(slot_ref, *refs):
    *recv_refs, win_ref, down_ref, up_ref, own_ref, cot_ref, cell_ref, tap_ref, block_ref = refs
    for n, k in enumerate(ORDER):
        block_ref[slot_ref[0] ^ k] = recv_refs[n][...]
    pixels = swap_blocks([block_ref[q, 0:80, :].astype(F32) for q in range(8)])
    for r in range(4):
        columns = (from_left(pixels[2 * r + 1]), pixels[2 * r], pixels[2 * r + 1])
        for b in range(3):
            part = columns[b].astype(BF16)
            for i in range(2):
                a = r + 1 - 2 * i
                if 0 <= a < 3:
                    t = 3 * a + b
                    win_ref[80 * t : 80 * t + 80, 128 * i : 128 * i + 128] = part
    win_ref[0:240, 0:128] = jnp.zeros((240, 128), BF16)
    down_ref[:, 0:128] = pixels[6].astype(BF16)
    down_ref[:, 128:256] = pixels[7].astype(BF16)
    for q in range(8):
        tap_ref[80 * q : 80 * q + 80, 0:128] = block_ref[q, 80:160, :]
        last = block_ref[q, 160:176, :].astype(F32)
        for b in range(5):
            moved = last if b == 0 else pltpu.roll(last, 128 - 16 * b, 1)
            tap_ref[80 * q + 16 * b : 80 * q + 16 * b + 16, 128:256] = moved.astype(BF16)
        for k in range(5):
            for i in range(2):
                start = 176 + 32 * k + 16 * i
                cell_ref[128 * i + 16 * q : 128 * i + 16 * q + 16, 128 * k : 128 * k + 128] = block_ref[q, start : start + 16, :]
    eye = jnp.where(iota((128, 128), 0) == iota((128, 128), 1), 1.0, 0.0).astype(BF16)
    for g in range(5):
        rows = slice(128 * g, 128 * g + 128)
        cot = nt(eye, cell_ref[:, rows]).astype(BF16)
        cot_ref[rows, :] = cot
        terms = tn(tap_ref[rows, :], cot)
        sums = []
        for u in range(3):
            base = 48 * u
            by_row = []
            for i in range(2):
                lanes = slice(128 * i, 128 * i + 128)
                by_row.append(
                    from_right(terms[base : base + 16, lanes])
                    + terms[base + 16 : base + 32, lanes]
                    + from_left(terms[base + 32 : base + 48, lanes])
                )
            sums.append(by_row)
        here = slice(16 * g, 16 * g + 16)
        own_ref[here, 0:128] = sums[1][0] + sums[0][1]
        own_ref[here, 128:256] = sums[1][1] + sums[2][0]
        up_ref[here, 0:128] = sums[0][0].astype(BF16)
        up_ref[here, 128:256] = recv_refs[0][176 + 32 * g : 192 + 32 * g, :]
        down_ref[here, 256:384] = sums[2][1].astype(BF16)
        down_ref[here, 384:512] = recv_refs[0][192 + 32 * g : 208 + 32 * g, :]


def forward_kernel(slot_ref, part_ref, down_ref, weight_ref, *refs):
    *hid_refs, win_ref, block_ref = refs
    odd = down_ref[:, 128:256]
    win_ref[...] = part_ref[...]
    win_ref[0:80, 0:128] = from_left(odd.astype(F32)).astype(BF16)
    win_ref[80:160, 0:128] = down_ref[:, 0:128]
    win_ref[160:240, 0:128] = odd
    hidden = tn(weight_ref[...], win_ref[...]).astype(BF16)
    for p in range(8):
        for g in range(5):
            block_ref[p, 16 * g : 16 * g + 16, :] = hidden[128 * g + 16 * p : 128 * g + 16 * p + 16]
    for n, k in enumerate(ORDER):
        hid_refs[n][...] = block_ref[slot_ref[0] ^ k]


def middle_kernel(own_ref, down_ref, up_ref, *refs):
    *hid_refs, act_ref, share_ref = refs
    hidden = hid_refs[0][...].astype(F32)
    for k in range(1, 8):
        hidden = hidden + hid_refs[k][...].astype(F32)
    cumul = 0.5 * (1.0 + lax.erf(hidden * (1.0 / math.sqrt(2.0))))
    density = jnp.exp(-0.5 * hidden * hidden) * (1.0 / math.sqrt(2.0 * math.pi))
    act_ref[...] = (hidden * cumul).astype(BF16)
    slopes = cumul + hidden * density
    act_grad = own_ref[...] + jnp.concatenate(
        [down_ref[:, 256:384].astype(F32), up_ref[:, 0:128].astype(F32)], axis=1
    )
    share_ref[0:80, :] = (act_grad * slopes).astype(BF16)
    share_ref[80:160, 0:128] = down_ref[:, 384:512]
    share_ref[80:160, 128:256] = up_ref[:, 128:256]


def weight_grad_kernel(all_ref, win_ref, cot_ref, act_ref, red_ref, pre_ref, shift_ref, cell_ref):
    for p in range(8):
        for g in range(5):
            pre_ref[128 * g + 16 * p : 128 * g + 16 * p + 16, :] = all_ref[p, 16 * g : 16 * g + 16, :]
    pre = pre_ref[...]
    red_ref[:, 0:640] = nt(pre, win_ref[0:640, :]).astype(BF16)
    rows = [act_ref[:, 128 * i : 128 * i + 128].astype(F32) for i in range(2)]
    moved = [[move(x).astype(BF16) for x in rows] for move in (from_left, lambda x: x, from_right)]
    shift_ref[...] = jnp.zeros((5, 256, 512), BF16)
    for g in range(5):
        for u in range(3):
            for v in range(3):
                base = 80 + 16 * (3 * u + v)
                for i in range(2):
                    lanes = slice(128 * (i + 2 - u), 128 * (i + 2 - u) + 128)
                    shift_ref[g, base : base + 16, lanes] = moved[v][i][16 * g : 16 * g + 16]
    for q in range(8):
        for k in range(5):
            for side in range(2):
                cell_ref[128 * side + 16 * q : 128 * side + 16 * q + 16, 128 * k : 128 * k + 128] = all_ref[
                    q, 80 + 16 * k : 96 + 16 * k, 128 * side : 128 * side + 128
                ]
    eye = jnp.where(iota((128, 128), 0) == iota((128, 128), 1), 1.0, 0.0).astype(BF16)
    tail = jnp.concatenate([win_ref[640:720, :], jnp.zeros((176, 256), BF16)], axis=0)
    last = nt(pre, tail)
    for g in range(5):
        here = slice(128 * g, 128 * g + 128)
        rims = nt(eye, cell_ref[:, here]).astype(BF16)
        cot = jnp.concatenate([rims[:, 0:128], cot_ref[here, :], rims[:, 128:256]], axis=1)
        red_ref[here, 640:896] = (last[here] + nt(cot, shift_ref[g])).astype(BF16)


def image_grad_kernel(pre_ref, weight_ref, img_ref, up_ref):
    pre = pre_ref[...]
    back = nn(weight_ref[...], pre)

    def term(a, b, i):
        t = 3 * a + b
        return back[80 * t : 80 * t + 80, 128 * i : 128 * i + 128]

    for i in range(2):
        img_ref[4 * i] = term(1, 1, i)
        img_ref[4 * i + 1] = term(1, 2, i) + from_right(term(1, 0, i))
    upper_even = [term(0, 1, i) for i in range(2)]
    upper_odd = [term(0, 2, i) + from_right(term(0, 0, i)) for i in range(2)]
    lower_odd = [term(2, 2, i) + from_right(term(2, 0, i)) for i in range(2)]
    img_ref[2] = term(2, 1, 0) + upper_even[1]
    img_ref[3] = lower_odd[0] + upper_odd[1]
    img_ref[6] = term(2, 1, 1)
    img_ref[7] = lower_odd[1]
    up_ref[0] = upper_even[0]
    up_ref[1] = upper_odd[0]


def return_kernel(slot_ref, img_ref, below_ref, *refs):
    *send_refs, slot_blocks = refs
    parts = [img_ref[k] for k in range(8)]
    parts[6] = parts[6] + below_ref[0]
    parts[7] = parts[7] + below_ref[1]
    for q, x in enumerate(swap_blocks(parts)):
        slot_blocks[slot_ref[0] ^ q] = x.astype(BF16)
    for n, k in enumerate(ORDER):
        send_refs[n][...] = slot_blocks[k]


def fold_kernel(high_ref, red_ref, keep_ref, give_ref):
    total = red_ref[0].astype(F32)
    for q in range(1, 16):
        total = total + red_ref[q].astype(F32)
    first, second = total[0:20], total[20:40]
    high = high_ref[0] == 1
    keep_ref[...] = jnp.where(high, second, first)
    give_ref[...] = jnp.where(high, first, second).astype(BF16)


def unpack_kernel(slot_ref, *refs):
    *recv_refs, out_ref, block_ref = refs
    for n, k in enumerate(ORDER):
        block_ref[slot_ref[0] ^ k] = recv_refs[n][...]
    lane = iota((128, 128), 1)
    pick = jnp.where(cell_of_lane(lane) == iota((128, 128), 0), 1.0, 0.0).astype(BF16)
    blocks = block_ref[...].reshape(640, 128)
    for p in range(5):
        out_ref[:, 128 * p : 128 * p + 128] = nt(pick, blocks[128 * p : 128 * p + 128]).astype(BF16)


def finish_kernel(keep_ref, given_ref, conv_ref, group_ref):
    total = keep_ref[...] + given_ref[...].astype(F32)
    for t in range(9):
        conv_ref[t] = total[:, 80 * t : 80 * t + 80]
    group_ref[...] = jnp.transpose(total[:, 640:896])[80:224]


def call(kernel, outs, *args, scratch=(), smem=0, flops=0):
    whole = [pl.BlockSpec(memory_space=pltpu.SMEM)] * smem
    whole += [pl.BlockSpec(memory_space=pltpu.VMEM)] * (len(args) - smem)
    return pl.pallas_call(
        kernel,
        out_shape=[jax.ShapeDtypeStruct(shape, dtype) for shape, dtype in outs],
        in_specs=whole,
        out_specs=[pl.BlockSpec(memory_space=pltpu.VMEM)] * len(outs),
        scratch_shapes=list(scratch),
        compiler_params=pltpu.CompilerParams(vmem_limit_bytes=48 * 1024 * 1024),
        cost_estimate=pl.CostEstimate(flops=flops, bytes_accessed=0, transcendentals=0) if flops else None,
    )(*args)


def trade(blocks):
    moved = [
        lax.ppermute(block, "fsdp", [(i, i ^ k) for i in range(8)])
        for k, block in zip(ORDER[1:], blocks[1:])
    ]
    return [blocks[0]] + moved


def per_device(image, conv_weight, group_weight, cotangent):
    tiles = lax.axis_size("tile")
    downward = [(i, i + 1) for i in range(tiles - 1)]
    upward = [(i + 1, i) for i in range(tiles - 1)]
    partners = [(i, i ^ 1) for i in range(tiles)]
    planes = [[2 * i + z for i in range(tiles // 2)] for z in range(2)]

    cells = cotangent.reshape(32, 640)
    slot = lax.axis_index("fsdp").astype(jnp.int32).reshape(1)
    weights = conv_weight.transpose(1, 0, 2).reshape(720, 640)
    parts = trade(
        call(
            pack_kernel, [((336, 128), BF16)] * 8,
            slot, image.reshape(128, 640), group_weight.transpose(0, 2, 1), cells,
            scratch=[pltpu.VMEM((8, 176, 128), BF16)], smem=1,
        )
    )
    windows, down, up, own, cot = call(
        spread_kernel,
        [((720, 256), BF16), ((80, 512), BF16), ((80, 256), BF16), ((80, 256), F32), ((640, 256), BF16)],
        slot, *parts,
        scratch=[pltpu.VMEM((256, 640), BF16), pltpu.VMEM((640, 256), BF16), pltpu.VMEM((8, 336, 128), BF16)],
        smem=1,
    )
    down = lax.ppermute(down, "tile", downward)
    *hid, windows = call(
        forward_kernel, [((80, 256), BF16)] * 8 + [((720, 256), BF16)],
        slot, windows, down, weights,
        scratch=[pltpu.VMEM((8, 80, 256), BF16)], smem=1, flops=FORWARD_FLOPS,
    )
    hid = trade(hid)
    up = lax.ppermute(up, "tile", upward)
    act, share = call(
        middle_kernel, [((80, 256), BF16), ((160, 256), BF16)], own, down, up, *hid
    )
    share_all = lax.all_gather(share, "fsdp", axis=0, tiled=False)
    red, pre = call(
        weight_grad_kernel,
        [((640, 896), BF16), ((640, 256), BF16)],
        share_all, windows, cot, act,
        scratch=[pltpu.VMEM((5, 256, 512), BF16), pltpu.VMEM((256, 640), BF16)],
    )
    img, img_up = call(
        image_grad_kernel, [((8, 80, 128), F32), ((2, 80, 128), F32)], pre, weights
    )
    img_below = lax.ppermute(img_up, "tile", upward)
    red = lax.all_to_all(
        red.reshape(16, 40, 896), "tile", 0, 0, tiled=True, axis_index_groups=planes
    )
    back = trade(
        call(
            return_kernel, [((80, 128), BF16)] * 8, slot, img, img_below,
            scratch=[pltpu.VMEM((8, 80, 128), BF16)], smem=1,
        )
    )
    high = (lax.axis_index("tile") % 2).astype(jnp.int32).reshape(1)
    keep, give = call(fold_kernel, [((20, 896), F32), ((20, 896), BF16)], high, red, smem=1)
    given = lax.ppermute(give, "tile", partners)
    (image_grad,) = call(
        unpack_kernel, [((128, 640), BF16)], slot, *back,
        scratch=[pltpu.VMEM((8, 80, 128), BF16)], smem=1,
    )
    conv_weight_grad, group_weight_grad = call(
        finish_kernel, [((9, 20, 80), F32), ((144, 20), F32)], keep, given
    )
    conv_weight_grad = conv_weight_grad.transpose(2, 0, 1)
    group_weight_grad = group_weight_grad.reshape(9, 16, 20)
    return (image_grad.reshape(4, 32, 640), conv_weight_grad, group_weight_grad)


def solution(mesh):
    placed = (
        P("tile", "fsdp", None),
        P("fsdp", None, None),
        P(None, None, "fsdp"),
        P("tile", "fsdp", None),
    )
    return jax.shard_map(
        per_device,
        mesh=mesh,
        in_specs=placed,
        out_specs=(P("tile", "fsdp", None), P("fsdp", None, "tile"), P(None, "fsdp", "tile")),
        check_vma=False,
    )
```

```python
import functools
import math

import jax
import jax.numpy as jnp
from jax import lax
from jax.experimental import pallas as pl
from jax.experimental.pallas import tpu as pltpu
from jax.sharding import PartitionSpec as P

F32 = jnp.float32
BF16 = jnp.bfloat16
ORDER = (0, 6, 4, 7, 5, 2, 3, 1)
GATHERED = (0, 6, 4, 2, 1, 7, 5, 3)
DIRECT = GATHERED[:5]
FORWARD_FLOPS = 12_000_000_000


def nn(a, b):
    return lax.dot_general(a, b, (((1,), (0,)), ((), ())), preferred_element_type=F32)


def nt(a, b):
    return lax.dot_general(a, b, (((1,), (1,)), ((), ())), preferred_element_type=F32)


def tn(a, b):
    return lax.dot_general(a, b, (((0,), (0,)), ((), ())), preferred_element_type=F32)


def iota(shape, dim):
    return lax.broadcasted_iota(jnp.int32, shape, dim)


def from_left(x):
    return jnp.where(iota(x.shape, 1) == 0, 0.0, pltpu.roll(x, 1, 1))


def from_right(x):
    width = x.shape[1]
    return jnp.where(iota(x.shape, 1) == width - 1, 0.0, pltpu.roll(x, width - 1, 1))


def swap_blocks(arrays):
    arrays = list(arrays)
    lane = iota(arrays[0].shape, 1) // 16
    for step in (1, 2, 4):
        upper = (lane & step) != 0
        for low in range(8):
            if low & step:
                continue
            a, b = arrays[low], arrays[low | step]
            arrays[low] = jnp.where(upper, pltpu.roll(b, 16 * step, 1), a)
            arrays[low | step] = jnp.where(upper, b, pltpu.roll(a, 128 - 16 * step, 1))
    return arrays


def cell_of_lane(lane):
    return (lane // 32) * 32 + 2 * (lane % 16) + (lane // 16) % 2


def pack_kernel(slot_ref, image_ref, group_ref, cot_ref, *refs):
    *send_refs, block_ref = refs
    pick = jnp.where(cell_of_lane(iota((128, 128), 1)) == iota((128, 128), 0), 1.0, 0.0)
    pixels = tn(image_ref[...], pick.astype(BF16)).astype(BF16)
    taps = swap_blocks([group_ref[t].astype(F32) for t in range(8)])
    last = [group_ref[8, 16 * b : 16 * b + 16, :].astype(F32) for b in range(5)]
    last = swap_blocks(last + [jnp.zeros((16, 128), F32)] * 3)
    for p in range(8):
        block_ref[p, 0:80, :] = pixels[80 * p : 80 * p + 80]
        block_ref[p, 80:160, :] = taps[p].astype(BF16)
        block_ref[p, 160:176, :] = last[p].astype(BF16)
    for n, k in enumerate(ORDER):
        send_refs[n][0:176, :] = block_ref[slot_ref[0] ^ k]
        for j in range(5 if k in DIRECT else 0):
            send_refs[n][176 + 32 * j : 208 + 32 * j, :] = cot_ref[:, 128 * j : 128 * j + 128]


def spread_kernel(slot_ref, *refs):
    *recv_refs, win_ref, down_ref, up_ref, own_ref, cot_ref, cell_ref, tap_ref, block_ref = refs
    for n, k in enumerate(ORDER):
        if k in DIRECT:
            block_ref[slot_ref[0] ^ k] = recv_refs[n][...]
        else:
            block_ref[slot_ref[0] ^ k, 0:176, :] = recv_refs[n][...]
            block_ref[slot_ref[0] ^ k, 176:336, :] = recv_refs[3 + GATHERED.index(k)][176:336, :]
    pixels = swap_blocks([block_ref[q, 0:80, :].astype(F32) for q in range(8)])
    for r in range(4):
        columns = (from_left(pixels[2 * r + 1]), pixels[2 * r], pixels[2 * r + 1])
        for b in range(3):
            part = columns[b].astype(BF16)
            for i in range(2):
                a = r + 1 - 2 * i
                if 0 <= a < 3:
                    t = 3 * a + b
                    win_ref[80 * t : 80 * t + 80, 128 * i : 128 * i + 128] = part
    win_ref[0:240, 0:128] = jnp.zeros((240, 128), BF16)
    down_ref[:, 0:128] = pixels[6].astype(BF16)
    down_ref[:, 128:256] = pixels[7].astype(BF16)
    for q in range(8):
        tap_ref[80 * q : 80 * q + 80, 0:128] = block_ref[q, 80:160, :]
        last = block_ref[q, 160:176, :].astype(F32)
        for b in range(5):
            moved = last if b == 0 else pltpu.roll(last, 128 - 16 * b, 1)
            tap_ref[80 * q + 16 * b : 80 * q + 16 * b + 16, 128:256] = moved.astype(BF16)
        for k in range(5):
            for i in range(2):
                start = 176 + 32 * k + 16 * i
                cell_ref[128 * i + 16 * q : 128 * i + 16 * q + 16, 128 * k : 128 * k + 128] = block_ref[q, start : start + 16, :]
    eye = jnp.where(iota((128, 128), 0) == iota((128, 128), 1), 1.0, 0.0).astype(BF16)
    for g in range(5):
        rows = slice(128 * g, 128 * g + 128)
        cot = nt(eye, cell_ref[:, rows]).astype(BF16)
        cot_ref[rows, :] = cot
        terms = tn(tap_ref[rows, :], cot)
        sums = []
        for u in range(3):
            base = 48 * u
            by_row = []
            for i in range(2):
                lanes = slice(128 * i, 128 * i + 128)
                by_row.append(
                    from_right(terms[base : base + 16, lanes])
                    + terms[base + 16 : base + 32, lanes]
                    + from_left(terms[base + 32 : base + 48, lanes])
                )
            sums.append(by_row)
        here = slice(16 * g, 16 * g + 16)
        own_ref[here, 0:128] = sums[1][0] + sums[0][1]
        own_ref[here, 128:256] = sums[1][1] + sums[2][0]
        up_ref[here, 0:128] = sums[0][0].astype(BF16)
        up_ref[here, 128:256] = recv_refs[0][176 + 32 * g : 192 + 32 * g, :]
        down_ref[here, 256:384] = sums[2][1].astype(BF16)
        down_ref[here, 384:512] = recv_refs[0][192 + 32 * g : 208 + 32 * g, :]


def forward_kernel(slot_ref, part_ref, down_ref, weight_ref, *refs):
    *hid_refs, win_ref, block_ref = refs
    odd = down_ref[:, 128:256]
    win_ref[...] = part_ref[...]
    win_ref[0:80, 0:128] = from_left(odd.astype(F32)).astype(BF16)
    win_ref[80:160, 0:128] = down_ref[:, 0:128]
    win_ref[160:240, 0:128] = odd
    hidden = tn(weight_ref[...], win_ref[...]).astype(BF16)
    for p in range(8):
        for g in range(5):
            block_ref[p, 16 * g : 16 * g + 16, :] = hidden[128 * g + 16 * p : 128 * g + 16 * p + 16]
    for n, k in enumerate(ORDER):
        hid_refs[n][...] = block_ref[slot_ref[0] ^ k]


def middle_kernel(own_ref, down_ref, up_ref, *refs):
    *hid_refs, act_ref, share_ref = refs
    hidden = hid_refs[0][...].astype(F32)
    for k in range(1, 8):
        hidden = hidden + hid_refs[k][...].astype(F32)
    cumul = 0.5 * (1.0 + lax.erf(hidden * (1.0 / math.sqrt(2.0))))
    density = jnp.exp(-0.5 * hidden * hidden) * (1.0 / math.sqrt(2.0 * math.pi))
    act_ref[...] = (hidden * cumul).astype(BF16)
    slopes = cumul + hidden * density
    act_grad = own_ref[...] + jnp.concatenate(
        [down_ref[:, 256:384].astype(F32), up_ref[:, 0:128].astype(F32)], axis=1
    )
    share_ref[0:80, :] = (act_grad * slopes).astype(BF16)
    share_ref[80:160, 0:128] = down_ref[:, 384:512]
    share_ref[80:160, 128:256] = up_ref[:, 128:256]


def weight_grad_kernel(slot_ref, win_ref, cot_ref, act_ref, *refs):
    *all_refs, red_ref, pre_ref, shift_ref, cell_ref = refs
    for n, k in enumerate(GATHERED):
        start = pl.multiple_of(16 * (slot_ref[0] ^ k), 16)
        for g in range(5):
            pre_ref[pl.ds(128 * g + start, 16), :] = all_refs[n][16 * g : 16 * g + 16, :]
            for side in range(2):
                cell_ref[pl.ds(128 * side + start, 16), 128 * g : 128 * g + 128] = all_refs[n][
                    80 + 16 * g : 96 + 16 * g, 128 * side : 128 * side + 128
                ]
    pre = pre_ref[...]
    red_ref[:, 0:640] = nt(pre, win_ref[0:640, :]).astype(BF16)
    rows = [act_ref[:, 128 * i : 128 * i + 128].astype(F32) for i in range(2)]
    moved = [[move(x).astype(BF16) for x in rows] for move in (from_left, lambda x: x, from_right)]
    shift_ref[...] = jnp.zeros((5, 256, 512), BF16)
    for g in range(5):
        for u in range(3):
            for v in range(3):
                base = 80 + 16 * (3 * u + v)
                for i in range(2):
                    lanes = slice(128 * (i + 2 - u), 128 * (i + 2 - u) + 128)
                    shift_ref[g, base : base + 16, lanes] = moved[v][i][16 * g : 16 * g + 16]
    eye = jnp.where(iota((128, 128), 0) == iota((128, 128), 1), 1.0, 0.0).astype(BF16)
    tail = jnp.concatenate([win_ref[640:720, :], jnp.zeros((176, 256), BF16)], axis=0)
    last = nt(pre, tail)
    for g in range(5):
        here = slice(128 * g, 128 * g + 128)
        rims = nt(eye, cell_ref[:, here]).astype(BF16)
        cot = jnp.concatenate([rims[:, 0:128], cot_ref[here, :], rims[:, 128:256]], axis=1)
        red_ref[here, 640:896] = (last[here] + nt(cot, shift_ref[g])).astype(BF16)


def image_grad_kernel(pre_ref, weight_ref, img_ref, up_ref):
    pre = pre_ref[...]
    back = nn(weight_ref[...], pre)

    def term(a, b, i):
        t = 3 * a + b
        return back[80 * t : 80 * t + 80, 128 * i : 128 * i + 128]

    for i in range(2):
        img_ref[4 * i] = term(1, 1, i)
        img_ref[4 * i + 1] = term(1, 2, i) + from_right(term(1, 0, i))
    upper_even = [term(0, 1, i) for i in range(2)]
    upper_odd = [term(0, 2, i) + from_right(term(0, 0, i)) for i in range(2)]
    lower_odd = [term(2, 2, i) + from_right(term(2, 0, i)) for i in range(2)]
    img_ref[2] = term(2, 1, 0) + upper_even[1]
    img_ref[3] = lower_odd[0] + upper_odd[1]
    img_ref[6] = term(2, 1, 1)
    img_ref[7] = lower_odd[1]
    up_ref[0] = upper_even[0].astype(BF16)
    up_ref[1] = upper_odd[0].astype(BF16)


def return_kernel(slot_ref, img_ref, below_ref, *refs):
    *send_refs, slot_blocks = refs
    parts = [img_ref[k] for k in range(8)]
    parts[6] = parts[6] + below_ref[0].astype(F32)
    parts[7] = parts[7] + below_ref[1].astype(F32)
    for q, x in enumerate(swap_blocks(parts)):
        slot_blocks[slot_ref[0] ^ q] = x.astype(BF16)
    for n, k in enumerate(ORDER):
        send_refs[n][...] = slot_blocks[k]


def fold_kernel(high_ref, red_ref, keep_ref, give_ref):
    total = red_ref[0].astype(F32)
    for q in range(1, 16):
        total = total + red_ref[q].astype(F32)
    first, second = total[0:20], total[20:40]
    high = high_ref[0] == 1
    keep_ref[...] = jnp.where(high, second, first)
    give_ref[...] = jnp.where(high, first, second).astype(BF16)


def unpack_kernel(slot_ref, *refs):
    *recv_refs, out_ref, block_ref = refs
    for n, k in enumerate(ORDER):
        block_ref[slot_ref[0] ^ k] = recv_refs[n][...]
    lane = iota((128, 128), 1)
    pick = jnp.where(cell_of_lane(lane) == iota((128, 128), 0), 1.0, 0.0).astype(BF16)
    blocks = block_ref[...].reshape(640, 128)
    for p in range(5):
        out_ref[:, 128 * p : 128 * p + 128] = nt(pick, blocks[128 * p : 128 * p + 128]).astype(BF16)


def finish_kernel(keep_ref, given_ref, conv_ref, group_ref):
    total = keep_ref[...] + given_ref[...].astype(F32)
    for t in range(9):
        conv_ref[t] = total[:, 80 * t : 80 * t + 80]
    group_ref[...] = jnp.transpose(total[:, 640:896])[80:224]


def call(kernel, outs, *args, scratch=(), smem=0, flops=0):
    whole = [pl.BlockSpec(memory_space=pltpu.SMEM)] * smem
    whole += [pl.BlockSpec(memory_space=pltpu.VMEM)] * (len(args) - smem)
    return pl.pallas_call(
        kernel,
        out_shape=[jax.ShapeDtypeStruct(shape, dtype) for shape, dtype in outs],
        in_specs=whole,
        out_specs=[pl.BlockSpec(memory_space=pltpu.VMEM)] * len(outs),
        scratch_shapes=list(scratch),
        compiler_params=pltpu.CompilerParams(vmem_limit_bytes=48 * 1024 * 1024),
        cost_estimate=pl.CostEstimate(flops=flops, bytes_accessed=0, transcendentals=0) if flops else None,
    )(*args)


def trade(blocks):
    moved = [
        lax.ppermute(block, "fsdp", [(i, i ^ k) for i in range(8)])
        for k, block in zip(ORDER[1:], blocks[1:])
    ]
    return [blocks[0]] + moved


def swap(block, k):
    return lax.ppermute(block, "fsdp", [(i, i ^ k) for i in range(8)])


def gather(block):
    direct = [swap(block, k) for k in GATHERED[1:5]]
    return [block] + direct + [swap(got, 1) for got in direct[:3]]


def per_device(image, conv_weight, group_weight, cotangent):
    tiles = lax.axis_size("tile")
    downward = [(i, i + 1) for i in range(tiles - 1)]
    upward = [(i + 1, i) for i in range(tiles - 1)]
    partners = [(i, i ^ 1) for i in range(tiles)]
    planes = [[2 * i + z for i in range(tiles // 2)] for z in range(2)]

    cells = cotangent.reshape(32, 640)
    slot = lax.axis_index("fsdp").astype(jnp.int32).reshape(1)
    weights = conv_weight.transpose(1, 0, 2).reshape(720, 640)
    parts = trade(
        call(
            pack_kernel, [((336 if k in DIRECT else 176, 128), BF16) for k in ORDER],
            slot, image.reshape(128, 640), group_weight.transpose(0, 2, 1), cells,
            scratch=[pltpu.VMEM((8, 176, 128), BF16)], smem=1,
        )
    )
    passed = [swap(parts[ORDER.index(k)], 1) for k in GATHERED[1:4]]
    windows, down, up, own, cot = call(
        spread_kernel,
        [((720, 256), BF16), ((80, 512), BF16), ((80, 256), BF16), ((80, 256), F32), ((640, 256), BF16)],
        slot, *parts, *passed,
        scratch=[pltpu.VMEM((256, 640), BF16), pltpu.VMEM((640, 256), BF16), pltpu.VMEM((8, 336, 128), BF16)],
        smem=1,
    )
    down = lax.ppermute(down, "tile", downward)
    *hid, windows = call(
        forward_kernel, [((80, 256), BF16)] * 8 + [((720, 256), BF16)],
        slot, windows, down, weights,
        scratch=[pltpu.VMEM((8, 80, 256), BF16)], smem=1, flops=FORWARD_FLOPS,
    )
    hid = trade(hid)
    up = lax.ppermute(up, "tile", upward)
    act, share = call(
        middle_kernel, [((80, 256), BF16), ((160, 256), BF16)], own, down, up, *hid
    )
    red, pre = call(
        weight_grad_kernel,
        [((640, 896), BF16), ((640, 256), BF16)],
        slot, windows, cot, act, *gather(share),
        scratch=[pltpu.VMEM((5, 256, 512), BF16), pltpu.VMEM((256, 640), BF16)], smem=1,
    )
    img, img_up = call(
        image_grad_kernel, [((8, 80, 128), F32), ((2, 80, 128), BF16)], pre, weights
    )
    img_below = lax.ppermute(img_up, "tile", upward)
    red = lax.all_to_all(
        red.reshape(16, 40, 896), "tile", 0, 0, tiled=True, axis_index_groups=planes
    )
    back = trade(
        call(
            return_kernel, [((80, 128), BF16)] * 8, slot, img, img_below,
            scratch=[pltpu.VMEM((8, 80, 128), BF16)], smem=1,
        )
    )
    high = (lax.axis_index("tile") % 2).astype(jnp.int32).reshape(1)
    keep, give = call(fold_kernel, [((20, 896), F32), ((20, 896), BF16)], high, red, smem=1)
    given = lax.ppermute(give, "tile", partners)
    (image_grad,) = call(
        unpack_kernel, [((128, 640), BF16)], slot, *back,
        scratch=[pltpu.VMEM((8, 80, 128), BF16)], smem=1,
    )
    conv_weight_grad, group_weight_grad = call(
        finish_kernel, [((9, 20, 80), F32), ((144, 20), F32)], keep, given
    )
    conv_weight_grad = conv_weight_grad.transpose(2, 0, 1)
    group_weight_grad = group_weight_grad.reshape(9, 16, 20)
    return (image_grad.reshape(4, 32, 640), conv_weight_grad, group_weight_grad)


def solution(mesh):
    placed = (
        P("tile", "fsdp", None),
        P("fsdp", None, None),
        P(None, None, "fsdp"),
        P("tile", "fsdp", None),
    )
    return jax.shard_map(
        per_device,
        mesh=mesh,
        in_specs=placed,
        out_specs=(P("tile", "fsdp", None), P("fsdp", None, "tile"), P(None, "fsdp", "tile")),
        check_vma=False,
    )
```

```python
import functools
import math

import jax
import jax.numpy as jnp
from jax import lax
from jax.experimental import pallas as pl
from jax.experimental.pallas import tpu as pltpu
from jax.sharding import PartitionSpec as P

F32 = jnp.float32
BF16 = jnp.bfloat16
SOURCE = (0, 2, 4, 6, 1, 3, 5, 7)
HEIGHTS = (80, 160, 160, 160, 80)
ORDER = (0, 6, 4, 7, 5, 2, 3, 1)
HEAVY = 12_000_000_000


def nn(a, b):
    return lax.dot_general(a, b, (((1,), (0,)), ((), ())), preferred_element_type=F32)


def nt(a, b):
    return lax.dot_general(a, b, (((1,), (1,)), ((), ())), preferred_element_type=F32)


def tn(a, b):
    return lax.dot_general(a, b, (((0,), (0,)), ((), ())), preferred_element_type=F32)


def iota(shape, dim):
    return lax.broadcasted_iota(jnp.int32, shape, dim)


def from_left(x):
    return jnp.where(iota(x.shape, 1) == 0, 0.0, pltpu.roll(x, 1, 1))


def from_right(x):
    width = x.shape[1]
    return jnp.where(iota(x.shape, 1) == width - 1, 0.0, pltpu.roll(x, width - 1, 1))


def swap_blocks(arrays):
    arrays = list(arrays)
    lane = iota(arrays[0].shape, 1) // 16
    for step in (1, 2, 4):
        upper = (lane & step) != 0
        for low in range(8):
            if low & step:
                continue
            a, b = arrays[low], arrays[low | step]
            arrays[low] = jnp.where(upper, pltpu.roll(b, 16 * step, 1), a)
            arrays[low | step] = jnp.where(upper, b, pltpu.roll(a, 128 - 16 * step, 1))
    return arrays


def cell_of_lane(lane):
    return (lane // 32) * 32 + 2 * (lane % 16) + (lane // 16) % 2


def pack_kernel(slot_ref, image_ref, group_ref, cot_ref, *refs):
    *send_refs, block_ref = refs
    pick = jnp.where(cell_of_lane(iota((128, 128), 1)) == iota((128, 128), 0), 1.0, 0.0)
    pixels = tn(image_ref[...], pick.astype(BF16)).astype(BF16)
    taps = swap_blocks([group_ref[t].astype(F32) for t in range(8)])
    last = [group_ref[8, 16 * b : 16 * b + 16, :].astype(F32) for b in range(5)]
    last = swap_blocks(last + [jnp.zeros((16, 128), F32)] * 3)
    for p in range(8):
        block_ref[p, 0:80, :] = pixels[80 * p : 80 * p + 80]
        block_ref[p, 80:160, :] = taps[p].astype(BF16)
        block_ref[p, 160:176, :] = last[p].astype(BF16)
    for n in range(5):
        send_refs[n][0:176, :] = block_ref[slot_ref[0] ^ SOURCE[n]]
        shared = 176
        if 0 < n < 4:
            send_refs[n][176:352, :] = block_ref[slot_ref[0] ^ SOURCE[n] ^ 1]
            shared = 352
        for j in range(5):
            start = shared + 32 * j
            send_refs[n][start : start + 32, :] = cot_ref[:, 128 * j : 128 * j + 128]


def spread_kernel(slot_ref, *refs):
    *recv_refs, win_ref, down_ref, up_ref, own_ref, cot_ref, cell_ref, tap_ref, block_ref = refs
    for n, k in enumerate(SOURCE):
        shared = 176 if n in (0, 4) else 352
        block_ref[slot_ref[0] ^ k, 0:176, :] = recv_refs[n][rows_for(n, 176), :]
        block_ref[slot_ref[0] ^ k, 176:336, :] = recv_refs[n][shared : shared + 160, :]
    pixels = swap_blocks([block_ref[q, 0:80, :].astype(F32) for q in range(8)])
    for r in range(4):
        columns = (from_left(pixels[2 * r + 1]), pixels[2 * r], pixels[2 * r + 1])
        for b in range(3):
            part = columns[b].astype(BF16)
            for i in range(2):
                a = r + 1 - 2 * i
                if 0 <= a < 3:
                    t = 3 * a + b
                    win_ref[80 * t : 80 * t + 80, 128 * i : 128 * i + 128] = part
    win_ref[0:240, 0:128] = jnp.zeros((240, 128), BF16)
    down_ref[:, 0:128] = pixels[6].astype(BF16)
    down_ref[:, 128:256] = pixels[7].astype(BF16)
    for q in range(8):
        tap_ref[80 * q : 80 * q + 80, 0:128] = block_ref[q, 80:160, :]
        last = block_ref[q, 160:176, :].astype(F32)
        for b in range(5):
            moved = last if b == 0 else pltpu.roll(last, 128 - 16 * b, 1)
            tap_ref[80 * q + 16 * b : 80 * q + 16 * b + 16, 128:256] = moved.astype(BF16)
        for k in range(5):
            for i in range(2):
                start = 176 + 32 * k + 16 * i
                cell_ref[128 * i + 16 * q : 128 * i + 16 * q + 16, 128 * k : 128 * k + 128] = block_ref[q, start : start + 16, :]
    eye = jnp.where(iota((128, 128), 0) == iota((128, 128), 1), 1.0, 0.0).astype(BF16)
    for g in range(5):
        rows = slice(128 * g, 128 * g + 128)
        cot = nt(eye, cell_ref[:, rows]).astype(BF16)
        cot_ref[rows, :] = cot
        terms = tn(tap_ref[rows, :], cot)
        sums = []
        for u in range(3):
            base = 48 * u
            by_row = []
            for i in range(2):
                lanes = slice(128 * i, 128 * i + 128)
                by_row.append(
                    from_right(terms[base : base + 16, lanes])
                    + terms[base + 16 : base + 32, lanes]
                    + from_left(terms[base + 32 : base + 48, lanes])
                )
            sums.append(by_row)
        here = slice(16 * g, 16 * g + 16)
        own_ref[here, 0:128] = sums[1][0] + sums[0][1]
        own_ref[here, 128:256] = sums[1][1] + sums[2][0]
        up_ref[here, 0:128] = sums[0][0].astype(BF16)
        up_ref[here, 128:256] = recv_refs[0][176 + 32 * g : 192 + 32 * g, :]
        down_ref[here, 256:384] = sums[2][1].astype(BF16)
        down_ref[here, 384:512] = recv_refs[0][192 + 32 * g : 208 + 32 * g, :]


def forward_kernel(slot_ref, part_ref, down_ref, weight_ref, *refs):
    *hid_refs, win_ref, block_ref = refs
    odd = down_ref[:, 128:256]
    win_ref[...] = part_ref[...]
    win_ref[0:80, 0:128] = from_left(odd.astype(F32)).astype(BF16)
    win_ref[80:160, 0:128] = down_ref[:, 0:128]
    win_ref[160:240, 0:128] = odd
    hidden = tn(weight_ref[...], win_ref[...]).astype(BF16)
    for p in range(8):
        for g in range(5):
            block_ref[p, 16 * g : 16 * g + 16, :] = hidden[128 * g + 16 * p : 128 * g + 16 * p + 16]
    for n, k in enumerate(ORDER):
        hid_refs[n][...] = block_ref[slot_ref[0] ^ k]


def middle_kernel(own_ref, down_ref, up_ref, *refs):
    *hid_refs, act_ref, share_ref = refs
    hidden = hid_refs[0][...].astype(F32)
    for n in range(1, 8):
        hidden = hidden + hid_refs[n][...].astype(F32)
    cumul = 0.5 * (1.0 + lax.erf(hidden * (1.0 / math.sqrt(2.0))))
    density = jnp.exp(-0.5 * hidden * hidden) * (1.0 / math.sqrt(2.0 * math.pi))
    act_ref[...] = (hidden * cumul).astype(BF16)
    slopes = cumul + hidden * density
    act_grad = own_ref[...] + jnp.concatenate(
        [down_ref[:, 256:384].astype(F32), up_ref[:, 0:128].astype(F32)], axis=1
    )
    share_ref[0:80, :] = (act_grad * slopes).astype(BF16)
    share_ref[80:160, 0:128] = down_ref[:, 384:512]
    share_ref[80:160, 128:256] = up_ref[:, 128:256]


def weight_grad_kernel(slot_ref, win_ref, cot_ref, act_ref, *refs):
    *all_refs, red_ref, pre_ref, shift_ref, cell_ref = refs
    for n, k in enumerate(SOURCE):
        start = pl.multiple_of(16 * (slot_ref[0] ^ k), 16)
        for g in range(5):
            pre_ref[pl.ds(128 * g + start, 16), :] = all_refs[n][16 * g : 16 * g + 16, :]
            for side in range(2):
                cell_ref[pl.ds(128 * side + start, 16), 128 * g : 128 * g + 128] = all_refs[n][
                    80 + 16 * g : 96 + 16 * g, 128 * side : 128 * side + 128
                ]
    pre = pre_ref[...]
    red_ref[:, 0:640] = nt(pre, win_ref[0:640, :]).astype(BF16)
    rows = [act_ref[:, 128 * i : 128 * i + 128].astype(F32) for i in range(2)]
    moved = [[move(x).astype(BF16) for x in rows] for move in (from_left, lambda x: x, from_right)]
    shift_ref[...] = jnp.zeros((5, 256, 512), BF16)
    for g in range(5):
        for u in range(3):
            for v in range(3):
                base = 80 + 16 * (3 * u + v)
                for i in range(2):
                    lanes = slice(128 * (i + 2 - u), 128 * (i + 2 - u) + 128)
                    shift_ref[g, base : base + 16, lanes] = moved[v][i][16 * g : 16 * g + 16]
    eye = jnp.where(iota((128, 128), 0) == iota((128, 128), 1), 1.0, 0.0).astype(BF16)
    tail = jnp.concatenate([win_ref[640:720, :], jnp.zeros((176, 256), BF16)], axis=0)
    last = nt(pre, tail)
    for g in range(5):
        here = slice(128 * g, 128 * g + 128)
        rims = nt(eye, cell_ref[:, here]).astype(BF16)
        cot = jnp.concatenate([rims[:, 0:128], cot_ref[here, :], rims[:, 128:256]], axis=1)
        red_ref[here, 640:896] = (last[here] + nt(cot, shift_ref[g])).astype(BF16)


def image_grad_kernel(pre_ref, weight_ref, img_ref, up_ref):
    pre = pre_ref[...]
    back = nn(weight_ref[...], pre)

    def term(a, b, i):
        t = 3 * a + b
        return back[80 * t : 80 * t + 80, 128 * i : 128 * i + 128]

    for i in range(2):
        img_ref[4 * i] = term(1, 1, i)
        img_ref[4 * i + 1] = term(1, 2, i) + from_right(term(1, 0, i))
    upper_even = [term(0, 1, i) for i in range(2)]
    upper_odd = [term(0, 2, i) + from_right(term(0, 0, i)) for i in range(2)]
    lower_odd = [term(2, 2, i) + from_right(term(2, 0, i)) for i in range(2)]
    img_ref[2] = term(2, 1, 0) + upper_even[1]
    img_ref[3] = lower_odd[0] + upper_odd[1]
    img_ref[6] = term(2, 1, 1)
    img_ref[7] = lower_odd[1]
    up_ref[0] = upper_even[0].astype(BF16)
    up_ref[1] = upper_odd[0].astype(BF16)


def return_kernel(slot_ref, img_ref, below_ref, *refs):
    *send_refs, slot_blocks = refs
    parts = [img_ref[k] for k in range(8)]
    parts[6] = parts[6] + below_ref[0].astype(F32)
    parts[7] = parts[7] + below_ref[1].astype(F32)
    for q, x in enumerate(swap_blocks(parts)):
        slot_blocks[q] = x.astype(BF16)
    for n in range(5):
        send_refs[n][0:80, :] = slot_blocks[slot_ref[0] ^ SOURCE[n]]
        if 0 < n < 4:
            send_refs[n][80:160, :] = slot_blocks[slot_ref[0] ^ SOURCE[n] ^ 1]


def fold_kernel(high_ref, red_ref, keep_ref, give_ref):
    total = red_ref[0].astype(F32)
    for q in range(1, 16):
        total = total + red_ref[q].astype(F32)
    first, second = total[0:20], total[20:40]
    high = high_ref[0] == 1
    keep_ref[...] = jnp.where(high, second, first)
    give_ref[...] = jnp.where(high, first, second).astype(BF16)


def join_kernel(keep_ref, own_ref, *refs):
    *line_refs, out_ref = refs
    out_ref[0:80, :] = own_ref[...]
    for n, line_ref in enumerate(line_refs):
        out_ref[80 * n + 80 : 80 * n + 160, :] = line_ref[80:160, :]


def unpack_kernel(slot_ref, *refs):
    *recv_refs, joined_ref, out_ref, token_ref, block_ref = refs
    token_ref[...] = joined_ref[0:16, :]
    for n in range(4):
        block_ref[slot_ref[0] ^ SOURCE[n]] = recv_refs[n][0:80, :]
        block_ref[slot_ref[0] ^ SOURCE[n] ^ 1] = joined_ref[80 * n : 80 * n + 80, :]
    lane = iota((128, 128), 1)
    pick = jnp.where(cell_of_lane(lane) == iota((128, 128), 0), 1.0, 0.0).astype(BF16)
    blocks = block_ref[...].reshape(640, 128)
    for p in range(5):
        out_ref[:, 128 * p : 128 * p + 128] = nt(pick, blocks[128 * p : 128 * p + 128]).astype(BF16)


def finish_kernel(keep_ref, given_ref, token_ref, conv_ref, group_ref):
    total = keep_ref[...] + given_ref[...].astype(F32)
    for t in range(9):
        conv_ref[t] = total[:, 80 * t : 80 * t + 80]
    group_ref[...] = jnp.transpose(total[:, 640:896])[80:224]


def call(kernel, outs, *args, scratch=(), smem=0, flops=0):
    whole = [pl.BlockSpec(memory_space=pltpu.SMEM)] * smem
    whole += [pl.BlockSpec(memory_space=pltpu.VMEM)] * (len(args) - smem)
    return pl.pallas_call(
        kernel,
        out_shape=[jax.ShapeDtypeStruct(shape, dtype) for shape, dtype in outs],
        in_specs=whole,
        out_specs=[pl.BlockSpec(memory_space=pltpu.VMEM)] * len(outs),
        scratch_shapes=list(scratch),
        compiler_params=pltpu.CompilerParams(vmem_limit_bytes=48 * 1024 * 1024),
        cost_estimate=pl.CostEstimate(flops=flops, bytes_accessed=0, transcendentals=0) if flops else None,
    )(*args)


def swap(block, k):
    return lax.ppermute(block, "fsdp", [(i, i ^ k) for i in range(8)])


def exchange(blocks):
    direct = [swap(block, k) for block, k in zip(blocks[1:], SOURCE[1:5])]
    return [blocks[0]] + direct + [swap(got, 1) for got in direct[:3]]


def rows_for(n, height):
    return slice(height, 2 * height) if n > 4 else slice(0, height)


def per_device(image, conv_weight, group_weight, cotangent):
    tiles = lax.axis_size("tile")
    downward = [(i, i + 1) for i in range(tiles - 1)]
    upward = [(i + 1, i) for i in range(tiles - 1)]
    partners = [(i, i ^ 1) for i in range(tiles)]
    planes = [[2 * i + z for i in range(tiles // 2)] for z in range(2)]

    cells = cotangent.reshape(32, 640)
    slot = lax.axis_index("fsdp").astype(jnp.int32).reshape(1)
    weights = conv_weight.transpose(1, 0, 2).reshape(720, 640)
    parts = exchange(
        call(
            pack_kernel, [((height, 128), BF16) for height in (336, 512, 512, 512, 336)],
            slot, image.reshape(128, 640), group_weight.transpose(0, 2, 1), cells,
            scratch=[pltpu.VMEM((8, 176, 128), BF16)], smem=1,
        )
    )
    windows, down, up, own, cot = call(
        spread_kernel,
        [((720, 256), BF16), ((80, 512), BF16), ((80, 256), BF16), ((80, 256), F32), ((640, 256), BF16)],
        slot, *parts,
        scratch=[pltpu.VMEM((256, 640), BF16), pltpu.VMEM((640, 256), BF16), pltpu.VMEM((8, 336, 128), BF16)],
        smem=1,
    )
    down = lax.ppermute(down, "tile", downward)
    *hid, windows = call(
        forward_kernel, [((80, 256), BF16)] * 8 + [((720, 256), BF16)],
        slot, windows, down, weights,
        scratch=[pltpu.VMEM((8, 80, 256), BF16)], smem=1, flops=HEAVY,
    )
    hid = [hid[0]] + [swap(block, k) for k, block in zip(ORDER[1:], hid[1:])]
    up = lax.ppermute(up, "tile", upward)
    act, share = call(
        middle_kernel, [((80, 256), BF16), ((160, 256), BF16)], own, down, up, *hid
    )
    red, pre = call(
        weight_grad_kernel,
        [((640, 896), BF16), ((640, 256), BF16)],
        slot, windows, cot, act, *exchange([share] * 5),
        scratch=[pltpu.VMEM((5, 256, 512), BF16), pltpu.VMEM((256, 640), BF16)], smem=1,
    )
    img, img_up = call(
        image_grad_kernel, [((8, 80, 128), F32), ((2, 80, 128), BF16)], pre, weights
    )
    img_below = lax.ppermute(img_up, "tile", upward)
    red = lax.all_to_all(
        red.reshape(16, 40, 896), "tile", 0, 0, tiled=True, axis_index_groups=planes
    )
    own, *others, core = call(
        return_kernel, [((height, 128), BF16) for height in HEIGHTS], slot, img, img_below,
        scratch=[pltpu.VMEM((8, 80, 128), BF16)], smem=1,
    )
    others = [swap(block, k) for block, k in zip(others, SOURCE[1:4])]
    high = (lax.axis_index("tile") % 2).astype(jnp.int32).reshape(1)
    keep, give = call(fold_kernel, [((20, 896), F32), ((20, 896), BF16)], high, red, smem=1)
    given = lax.ppermute(give, "tile", partners)
    (core,) = call(join_kernel, [((320, 128), BF16)], keep, core, *others)
    core = swap(core, 1)
    image_grad, token = call(
        unpack_kernel, [((128, 640), BF16), ((16, 128), BF16)], slot, own, *others, core,
        scratch=[pltpu.VMEM((8, 80, 128), BF16)], smem=1,
    )
    conv_weight_grad, group_weight_grad = call(
        finish_kernel, [((9, 20, 80), F32), ((144, 20), F32)], keep, given, token
    )
    conv_weight_grad = conv_weight_grad.transpose(2, 0, 1)
    group_weight_grad = group_weight_grad.reshape(9, 16, 20)
    return (image_grad.reshape(4, 32, 640), conv_weight_grad, group_weight_grad)


def solution(mesh):
    placed = (
        P("tile", "fsdp", None),
        P("fsdp", None, None),
        P(None, None, "fsdp"),
        P("tile", "fsdp", None),
    )
    return jax.shard_map(
        per_device,
        mesh=mesh,
        in_specs=placed,
        out_specs=(P("tile", "fsdp", None), P("fsdp", None, "tile"), P(None, "fsdp", "tile")),
        check_vma=False,
    )
```

```python
import functools
import math

import jax
import jax.numpy as jnp
from jax import lax
from jax.experimental import pallas as pl
from jax.experimental.pallas import tpu as pltpu
from jax.sharding import PartitionSpec as P

F32 = jnp.float32
BF16 = jnp.bfloat16
SOURCE = (0, 6, 4, 2, 1, 7, 5, 3)
GATHERED = (0, 2, 4, 6, 1, 3, 5, 7)
HEIGHTS = (80, 160, 160, 160, 80)
ORDER = (0, 6, 4, 7, 5, 2, 3, 1)
HEAVY = 12_000_000_000


def nn(a, b):
    return lax.dot_general(a, b, (((1,), (0,)), ((), ())), preferred_element_type=F32)


def nt(a, b):
    return lax.dot_general(a, b, (((1,), (1,)), ((), ())), preferred_element_type=F32)


def tn(a, b):
    return lax.dot_general(a, b, (((0,), (0,)), ((), ())), preferred_element_type=F32)


def iota(shape, dim):
    return lax.broadcasted_iota(jnp.int32, shape, dim)


def from_left(x):
    return jnp.where(iota(x.shape, 1) == 0, 0.0, pltpu.roll(x, 1, 1))


def from_right(x):
    width = x.shape[1]
    return jnp.where(iota(x.shape, 1) == width - 1, 0.0, pltpu.roll(x, width - 1, 1))


def swap_blocks(arrays):
    arrays = list(arrays)
    lane = iota(arrays[0].shape, 1) // 16
    for step in (1, 2, 4):
        upper = (lane & step) != 0
        for low in range(8):
            if low & step:
                continue
            a, b = arrays[low], arrays[low | step]
            arrays[low] = jnp.where(upper, pltpu.roll(b, 16 * step, 1), a)
            arrays[low | step] = jnp.where(upper, b, pltpu.roll(a, 128 - 16 * step, 1))
    return arrays


def cell_of_lane(lane):
    return (lane // 32) * 32 + 2 * (lane % 16) + (lane // 16) % 2


def pack_kernel(slot_ref, image_ref, group_ref, cot_ref, *refs):
    *send_refs, block_ref = refs
    pick = jnp.where(cell_of_lane(iota((128, 128), 1)) == iota((128, 128), 0), 1.0, 0.0)
    pixels = tn(image_ref[...], pick.astype(BF16)).astype(BF16)
    taps = swap_blocks([group_ref[t].astype(F32) for t in range(8)])
    last = [group_ref[8, 16 * b : 16 * b + 16, :].astype(F32) for b in range(5)]
    last = swap_blocks(last + [jnp.zeros((16, 128), F32)] * 3)
    for p in range(8):
        block_ref[p, 0:80, :] = pixels[80 * p : 80 * p + 80]
        block_ref[p, 80:160, :] = taps[p].astype(BF16)
        block_ref[p, 160:176, :] = last[p].astype(BF16)
    for n in range(5):
        send_refs[n][0:176, :] = block_ref[slot_ref[0] ^ SOURCE[n]]
        shared = 176
        if 0 < n < 4:
            send_refs[n][176:352, :] = block_ref[slot_ref[0] ^ SOURCE[n] ^ 1]
            shared = 352
        for j in range(5):
            start = shared + 32 * j
            send_refs[n][start : start + 32, :] = cot_ref[:, 128 * j : 128 * j + 128]


def spread_kernel(slot_ref, *refs):
    *recv_refs, win_ref, down_ref, up_ref, own_ref, cot_ref, cell_ref, tap_ref, block_ref = refs
    for n, k in enumerate(SOURCE):
        shared = 176 if n in (0, 4) else 352
        block_ref[slot_ref[0] ^ k, 0:176, :] = recv_refs[n][rows_for(n, 176), :]
        block_ref[slot_ref[0] ^ k, 176:336, :] = recv_refs[n][shared : shared + 160, :]
    pixels = swap_blocks([block_ref[q, 0:80, :].astype(F32) for q in range(8)])
    for r in range(4):
        columns = (from_left(pixels[2 * r + 1]), pixels[2 * r], pixels[2 * r + 1])
        for b in range(3):
            part = columns[b].astype(BF16)
            for i in range(2):
                a = r + 1 - 2 * i
                if 0 <= a < 3:
                    t = 3 * a + b
                    win_ref[80 * t : 80 * t + 80, 128 * i : 128 * i + 128] = part
    win_ref[0:240, 0:128] = jnp.zeros((240, 128), BF16)
    down_ref[:, 0:128] = pixels[6].astype(BF16)
    down_ref[:, 128:256] = pixels[7].astype(BF16)
    for q in range(8):
        tap_ref[80 * q : 80 * q + 80, 0:128] = block_ref[q, 80:160, :]
        last = block_ref[q, 160:176, :].astype(F32)
        for b in range(5):
            moved = last if b == 0 else pltpu.roll(last, 128 - 16 * b, 1)
            tap_ref[80 * q + 16 * b : 80 * q + 16 * b + 16, 128:256] = moved.astype(BF16)
        for k in range(5):
            for i in range(2):
                start = 176 + 32 * k + 16 * i
                cell_ref[128 * i + 16 * q : 128 * i + 16 * q + 16, 128 * k : 128 * k + 128] = block_ref[q, start : start + 16, :]
    eye = jnp.where(iota((128, 128), 0) == iota((128, 128), 1), 1.0, 0.0).astype(BF16)
    for g in range(5):
        rows = slice(128 * g, 128 * g + 128)
        cot = nt(eye, cell_ref[:, rows]).astype(BF16)
        cot_ref[rows, :] = cot
        terms = tn(tap_ref[rows, :], cot)
        sums = []
        for u in range(3):
            base = 48 * u
            by_row = []
            for i in range(2):
                lanes = slice(128 * i, 128 * i + 128)
                by_row.append(
                    from_right(terms[base : base + 16, lanes])
                    + terms[base + 16 : base + 32, lanes]
                    + from_left(terms[base + 32 : base + 48, lanes])
                )
            sums.append(by_row)
        here = slice(16 * g, 16 * g + 16)
        own_ref[here, 0:128] = sums[1][0] + sums[0][1]
        own_ref[here, 128:256] = sums[1][1] + sums[2][0]
        up_ref[here, 0:128] = sums[0][0].astype(BF16)
        up_ref[here, 128:256] = recv_refs[0][176 + 32 * g : 192 + 32 * g, :]
        down_ref[here, 256:384] = sums[2][1].astype(BF16)
        down_ref[here, 384:512] = recv_refs[0][192 + 32 * g : 208 + 32 * g, :]


def forward_kernel(slot_ref, part_ref, down_ref, weight_ref, *refs):
    *hid_refs, win_ref, block_ref = refs
    odd = down_ref[:, 128:256]
    win_ref[...] = part_ref[...]
    win_ref[0:80, 0:128] = from_left(odd.astype(F32)).astype(BF16)
    win_ref[80:160, 0:128] = down_ref[:, 0:128]
    win_ref[160:240, 0:128] = odd
    hidden = tn(weight_ref[...], win_ref[...]).astype(BF16)
    for p in range(8):
        for g in range(5):
            block_ref[p, 16 * g : 16 * g + 16, :] = hidden[128 * g + 16 * p : 128 * g + 16 * p + 16]
    for n, k in enumerate(ORDER):
        hid_refs[n][...] = block_ref[slot_ref[0] ^ k]


def middle_kernel(own_ref, down_ref, up_ref, *refs):
    *hid_refs, act_ref, share_ref = refs
    hidden = hid_refs[0][...].astype(F32)
    for n in range(1, 8):
        hidden = hidden + hid_refs[n][...].astype(F32)
    cumul = 0.5 * (1.0 + lax.erf(hidden * (1.0 / math.sqrt(2.0))))
    density = jnp.exp(-0.5 * hidden * hidden) * (1.0 / math.sqrt(2.0 * math.pi))
    act_ref[...] = (hidden * cumul).astype(BF16)
    slopes = cumul + hidden * density
    act_grad = own_ref[...] + jnp.concatenate(
        [down_ref[:, 256:384].astype(F32), up_ref[:, 0:128].astype(F32)], axis=1
    )
    share_ref[0:80, :] = (act_grad * slopes).astype(BF16)
    share_ref[80:160, 0:128] = down_ref[:, 384:512]
    share_ref[80:160, 128:256] = up_ref[:, 128:256]


def group_grad_kernel(act_ref, cot_ref, part_ref, edge_ref, inner_ref):
    rows = [act_ref[:, 128 * i : 128 * i + 128].astype(F32) for i in range(2)]
    moved = [[move(x).astype(BF16) for x in rows] for move in (from_left, lambda x: x, from_right)]
    edge_ref[...] = jnp.zeros((5, 256, 256), BF16)
    inner_ref[...] = jnp.zeros((5, 256, 256), BF16)
    for g in range(5):
        for u in range(3):
            for v in range(3):
                base = 80 + 16 * (3 * u + v)
                for i in range(2):
                    row = i + 1 - u
                    target_ref = inner_ref if 0 <= row < 2 else edge_ref
                    lanes = slice(0, 128) if row in (0, -1) else slice(128, 256)
                    target_ref[g, base : base + 16, lanes] = moved[v][i][16 * g : 16 * g + 16]
    for g in range(5):
        here = slice(128 * g, 128 * g + 128)
        part_ref[here, :] = nt(cot_ref[here, :], inner_ref[g])


def weight_grad_kernel(slot_ref, win_ref, part_ref, shift_ref, *refs):
    *all_refs, red_ref, pre_ref, cell_ref = refs
    for n, k in enumerate(GATHERED):
        start = pl.multiple_of(16 * (slot_ref[0] ^ k), 16)
        for g in range(5):
            pre_ref[pl.ds(128 * g + start, 16), :] = all_refs[n][16 * g : 16 * g + 16, :]
            for side in range(2):
                cell_ref[pl.ds(128 * side + start, 16), 128 * g : 128 * g + 128] = all_refs[n][
                    80 + 16 * g : 96 + 16 * g, 128 * side : 128 * side + 128
                ]
    pre = pre_ref[...]
    red_ref[:, 0:640] = nt(pre, win_ref[0:640, :]).astype(BF16)
    eye = jnp.where(iota((128, 128), 0) == iota((128, 128), 1), 1.0, 0.0).astype(BF16)
    tail = jnp.concatenate([win_ref[640:720, :], jnp.zeros((176, 256), BF16)], axis=0)
    last = nt(pre, tail)
    for g in range(5):
        here = slice(128 * g, 128 * g + 128)
        rims = nt(eye, cell_ref[:, here]).astype(BF16)
        group = part_ref[here, :] + nt(rims, shift_ref[g])
        red_ref[here, 640:896] = (last[here] + group).astype(BF16)


def image_grad_kernel(pre_ref, weight_ref, img_ref, up_ref):
    pre = pre_ref[...]
    back = nn(weight_ref[...], pre)

    def term(a, b, i):
        t = 3 * a + b
        return back[80 * t : 80 * t + 80, 128 * i : 128 * i + 128]

    for i in range(2):
        img_ref[4 * i] = term(1, 1, i)
        img_ref[4 * i + 1] = term(1, 2, i) + from_right(term(1, 0, i))
    upper_even = [term(0, 1, i) for i in range(2)]
    upper_odd = [term(0, 2, i) + from_right(term(0, 0, i)) for i in range(2)]
    lower_odd = [term(2, 2, i) + from_right(term(2, 0, i)) for i in range(2)]
    img_ref[2] = term(2, 1, 0) + upper_even[1]
    img_ref[3] = lower_odd[0] + upper_odd[1]
    img_ref[6] = term(2, 1, 1)
    img_ref[7] = lower_odd[1]
    up_ref[0] = upper_even[0].astype(BF16)
    up_ref[1] = upper_odd[0].astype(BF16)


def return_kernel(slot_ref, img_ref, below_ref, *refs):
    *send_refs, slot_blocks = refs
    parts = [img_ref[k] for k in range(8)]
    parts[6] = parts[6] + below_ref[0].astype(F32)
    parts[7] = parts[7] + below_ref[1].astype(F32)
    for q, x in enumerate(swap_blocks(parts)):
        slot_blocks[q] = x.astype(BF16)
    for n in range(5):
        send_refs[n][0:80, :] = slot_blocks[slot_ref[0] ^ SOURCE[n]]
        if 0 < n < 4:
            send_refs[n][80:160, :] = slot_blocks[slot_ref[0] ^ SOURCE[n] ^ 1]


def fold_kernel(high_ref, red_ref, keep_ref, give_ref):
    total = red_ref[0].astype(F32)
    for q in range(1, 16):
        total = total + red_ref[q].astype(F32)
    first, second = total[0:20], total[20:40]
    high = high_ref[0] == 1
    keep_ref[...] = jnp.where(high, second, first)
    give_ref[...] = jnp.where(high, first, second).astype(BF16)


def join_kernel(keep_ref, own_ref, *refs):
    *line_refs, out_ref = refs
    out_ref[0:80, :] = own_ref[...]
    for n, line_ref in enumerate(line_refs):
        out_ref[80 * n + 80 : 80 * n + 160, :] = line_ref[80:160, :]


def unpack_kernel(slot_ref, *refs):
    *recv_refs, joined_ref, out_ref, token_ref, block_ref = refs
    token_ref[...] = joined_ref[0:16, :]
    for n in range(4):
        block_ref[slot_ref[0] ^ SOURCE[n]] = recv_refs[n][0:80, :]
        block_ref[slot_ref[0] ^ SOURCE[n] ^ 1] = joined_ref[80 * n : 80 * n + 80, :]
    lane = iota((128, 128), 1)
    pick = jnp.where(cell_of_lane(lane) == iota((128, 128), 0), 1.0, 0.0).astype(BF16)
    blocks = block_ref[...].reshape(640, 128)
    for p in range(5):
        out_ref[:, 128 * p : 128 * p + 128] = nt(pick, blocks[128 * p : 128 * p + 128]).astype(BF16)


def finish_kernel(keep_ref, given_ref, token_ref, conv_ref, group_ref):
    total = keep_ref[...] + given_ref[...].astype(F32)
    for t in range(9):
        conv_ref[t] = total[:, 80 * t : 80 * t + 80]
    group_ref[...] = jnp.transpose(total[:, 640:896])[80:224]


def call(kernel, outs, *args, scratch=(), smem=0, flops=0):
    whole = [pl.BlockSpec(memory_space=pltpu.SMEM)] * smem
    whole += [pl.BlockSpec(memory_space=pltpu.VMEM)] * (len(args) - smem)
    return pl.pallas_call(
        kernel,
        out_shape=[jax.ShapeDtypeStruct(shape, dtype) for shape, dtype in outs],
        in_specs=whole,
        out_specs=[pl.BlockSpec(memory_space=pltpu.VMEM)] * len(outs),
        scratch_shapes=list(scratch),
        compiler_params=pltpu.CompilerParams(vmem_limit_bytes=48 * 1024 * 1024),
        cost_estimate=pl.CostEstimate(flops=flops, bytes_accessed=0, transcendentals=0) if flops else None,
    )(*args)


def swap(block, k):
    return lax.ppermute(block, "fsdp", [(i, i ^ k) for i in range(8)])


def exchange(blocks, source=SOURCE):
    direct = [swap(block, k) for block, k in zip(blocks[1:], source[1:5])]
    return [blocks[0]] + direct + [swap(got, 1) for got in direct[:3]]


def rows_for(n, height):
    return slice(height, 2 * height) if n > 4 else slice(0, height)


def per_device(image, conv_weight, group_weight, cotangent):
    tiles = lax.axis_size("tile")
    downward = [(i, i + 1) for i in range(tiles - 1)]
    upward = [(i + 1, i) for i in range(tiles - 1)]
    partners = [(i, i ^ 1) for i in range(tiles)]
    planes = [[2 * i + z for i in range(tiles // 2)] for z in range(2)]

    cells = cotangent.reshape(32, 640)
    slot = lax.axis_index("fsdp").astype(jnp.int32).reshape(1)
    weights = conv_weight.transpose(1, 0, 2).reshape(720, 640)
    parts = exchange(
        call(
            pack_kernel, [((height, 128), BF16) for height in (336, 512, 512, 512, 336)],
            slot, image.reshape(128, 640), group_weight.transpose(0, 2, 1), cells,
            scratch=[pltpu.VMEM((8, 176, 128), BF16)], smem=1,
        )
    )
    windows, down, up, own, cot = call(
        spread_kernel,
        [((720, 256), BF16), ((80, 512), BF16), ((80, 256), BF16), ((80, 256), F32), ((640, 256), BF16)],
        slot, *parts,
        scratch=[pltpu.VMEM((256, 640), BF16), pltpu.VMEM((640, 256), BF16), pltpu.VMEM((8, 336, 128), BF16)],
        smem=1,
    )
    down = lax.ppermute(down, "tile", downward)
    *hid, windows = call(
        forward_kernel, [((80, 256), BF16)] * 8 + [((720, 256), BF16)],
        slot, windows, down, weights,
        scratch=[pltpu.VMEM((8, 80, 256), BF16)], smem=1, flops=HEAVY,
    )
    hid = [hid[0]] + [swap(block, k) for k, block in zip(ORDER[1:], hid[1:])]
    up = lax.ppermute(up, "tile", upward)
    act, share = call(
        middle_kernel, [((80, 256), BF16), ((160, 256), BF16)], own, down, up, *hid
    )
    part, edge = call(
        group_grad_kernel, [((640, 256), F32), ((5, 256, 256), BF16)], act, cot,
        scratch=[pltpu.VMEM((5, 256, 256), BF16)],
    )
    red, pre = call(
        weight_grad_kernel,
        [((640, 896), BF16), ((640, 256), BF16)],
        slot, windows, part, edge, *exchange([share] * 5, GATHERED),
        scratch=[pltpu.VMEM((256, 640), BF16)], smem=1,
    )
    img, img_up = call(
        image_grad_kernel, [((8, 80, 128), F32), ((2, 80, 128), BF16)], pre, weights
    )
    img_below = lax.ppermute(img_up, "tile", upward)
    red = lax.all_to_all(
        red.reshape(16, 40, 896), "tile", 0, 0, tiled=True, axis_index_groups=planes
    )
    own, *others, core = call(
        return_kernel, [((height, 128), BF16) for height in HEIGHTS], slot, img, img_below,
        scratch=[pltpu.VMEM((8, 80, 128), BF16)], smem=1,
    )
    others = [swap(block, k) for block, k in zip(others, SOURCE[1:4])]
    high = (lax.axis_index("tile") % 2).astype(jnp.int32).reshape(1)
    keep, give = call(fold_kernel, [((20, 896), F32), ((20, 896), BF16)], high, red, smem=1)
    given = lax.ppermute(give, "tile", partners)
    (core,) = call(join_kernel, [((320, 128), BF16)], keep, core, *others)
    core = swap(core, 1)
    image_grad, token = call(
        unpack_kernel, [((128, 640), BF16), ((16, 128), BF16)], slot, own, *others, core,
        scratch=[pltpu.VMEM((8, 80, 128), BF16)], smem=1,
    )
    conv_weight_grad, group_weight_grad = call(
        finish_kernel, [((9, 20, 80), F32), ((144, 20), F32)], keep, given, token
    )
    conv_weight_grad = conv_weight_grad.transpose(2, 0, 1)
    group_weight_grad = group_weight_grad.reshape(9, 16, 20)
    return (image_grad.reshape(4, 32, 640), conv_weight_grad, group_weight_grad)


def solution(mesh):
    placed = (
        P("tile", "fsdp", None),
        P("fsdp", None, None),
        P(None, None, "fsdp"),
        P("tile", "fsdp", None),
    )
    return jax.shard_map(
        per_device,
        mesh=mesh,
        in_specs=placed,
        out_specs=(P("tile", "fsdp", None), P("fsdp", None, "tile"), P(None, "fsdp", "tile")),
        check_vma=False,
    )
```

```python
import functools
import math

import jax
import jax.numpy as jnp
from jax import lax
from jax.experimental import pallas as pl
from jax.experimental.pallas import tpu as pltpu
from jax.sharding import PartitionSpec as P

F32 = jnp.float32
BF16 = jnp.bfloat16
SOURCE = (0, 6, 4, 2, 1, 7, 5, 3)
GATHERED = (0, 2, 4, 6, 1, 3, 5, 7)
HEIGHTS = (80, 160, 160, 160, 80)
ORDER = (0, 4, 6, 5, 7, 2, 3, 1)
HEAVY = 12_000_000_000


def nn(a, b):
    return lax.dot_general(a, b, (((1,), (0,)), ((), ())), preferred_element_type=F32)


def nt(a, b):
    return lax.dot_general(a, b, (((1,), (1,)), ((), ())), preferred_element_type=F32)


def tn(a, b):
    return lax.dot_general(a, b, (((0,), (0,)), ((), ())), preferred_element_type=F32)


def iota(shape, dim):
    return lax.broadcasted_iota(jnp.int32, shape, dim)


def from_left(x):
    return jnp.where(iota(x.shape, 1) == 0, 0.0, pltpu.roll(x, 1, 1))


def from_right(x):
    width = x.shape[1]
    return jnp.where(iota(x.shape, 1) == width - 1, 0.0, pltpu.roll(x, width - 1, 1))


def swap_blocks(arrays):
    arrays = list(arrays)
    lane = iota(arrays[0].shape, 1) // 16
    for step in (1, 2, 4):
        upper = (lane & step) != 0
        for low in range(8):
            if low & step:
                continue
            a, b = arrays[low], arrays[low | step]
            arrays[low] = jnp.where(upper, pltpu.roll(b, 16 * step, 1), a)
            arrays[low | step] = jnp.where(upper, b, pltpu.roll(a, 128 - 16 * step, 1))
    return arrays


def cell_of_lane(lane):
    return (lane // 32) * 32 + 2 * (lane % 16) + (lane // 16) % 2


def pack_kernel(slot_ref, image_ref, group_ref, cot_ref, *refs):
    *send_refs, block_ref = refs
    pick = jnp.where(cell_of_lane(iota((128, 128), 1)) == iota((128, 128), 0), 1.0, 0.0)
    pixels = tn(image_ref[...], pick.astype(BF16)).astype(BF16)
    taps = swap_blocks([group_ref[t].astype(F32) for t in range(8)])
    last = [group_ref[8, 16 * b : 16 * b + 16, :].astype(F32) for b in range(5)]
    last = swap_blocks(last + [jnp.zeros((16, 128), F32)] * 3)
    for p in range(8):
        block_ref[p, 0:80, :] = pixels[80 * p : 80 * p + 80]
        block_ref[p, 80:160, :] = taps[p].astype(BF16)
        block_ref[p, 160:176, :] = last[p].astype(BF16)
    for n in range(5):
        send_refs[n][0:176, :] = block_ref[slot_ref[0] ^ SOURCE[n]]
        shared = 176
        if 0 < n < 4:
            send_refs[n][176:352, :] = block_ref[slot_ref[0] ^ SOURCE[n] ^ 1]
            shared = 352
        for j in range(5):
            start = shared + 32 * j
            send_refs[n][start : start + 32, :] = cot_ref[:, 128 * j : 128 * j + 128]


def spread_kernel(slot_ref, *refs):
    *recv_refs, win_ref, down_ref, up_ref, own_ref, cot_ref, cell_ref, tap_ref, block_ref = refs
    for n, k in enumerate(SOURCE):
        shared = 176 if n in (0, 4) else 352
        block_ref[slot_ref[0] ^ k, 0:176, :] = recv_refs[n][rows_for(n, 176), :]
        block_ref[slot_ref[0] ^ k, 176:336, :] = recv_refs[n][shared : shared + 160, :]
    pixels = swap_blocks([block_ref[q, 0:80, :].astype(F32) for q in range(8)])
    for r in range(4):
        columns = (from_left(pixels[2 * r + 1]), pixels[2 * r], pixels[2 * r + 1])
        for b in range(3):
            part = columns[b].astype(BF16)
            for i in range(2):
                a = r + 1 - 2 * i
                if 0 <= a < 3:
                    t = 3 * a + b
                    win_ref[80 * t : 80 * t + 80, 128 * i : 128 * i + 128] = part
    win_ref[0:240, 0:128] = jnp.zeros((240, 128), BF16)
    down_ref[:, 0:128] = pixels[6].astype(BF16)
    down_ref[:, 128:256] = pixels[7].astype(BF16)
    for q in range(8):
        tap_ref[80 * q : 80 * q + 80, 0:128] = block_ref[q, 80:160, :]
        last = block_ref[q, 160:176, :].astype(F32)
        for b in range(5):
            moved = last if b == 0 else pltpu.roll(last, 128 - 16 * b, 1)
            tap_ref[80 * q + 16 * b : 80 * q + 16 * b + 16, 128:256] = moved.astype(BF16)
        for k in range(5):
            for i in range(2):
                start = 176 + 32 * k + 16 * i
                cell_ref[128 * i + 16 * q : 128 * i + 16 * q + 16, 128 * k : 128 * k + 128] = block_ref[q, start : start + 16, :]
    eye = jnp.where(iota((128, 128), 0) == iota((128, 128), 1), 1.0, 0.0).astype(BF16)
    for g in range(5):
        rows = slice(128 * g, 128 * g + 128)
        cot = nt(eye, cell_ref[:, rows]).astype(BF16)
        cot_ref[rows, :] = cot
        terms = tn(tap_ref[rows, :], cot)
        sums = []
        for u in range(3):
            base = 48 * u
            by_row = []
            for i in range(2):
                lanes = slice(128 * i, 128 * i + 128)
                by_row.append(
                    from_right(terms[base : base + 16, lanes])
                    + terms[base + 16 : base + 32, lanes]
                    + from_left(terms[base + 32 : base + 48, lanes])
                )
            sums.append(by_row)
        here = slice(16 * g, 16 * g + 16)
        own_ref[here, 0:128] = sums[1][0] + sums[0][1]
        own_ref[here, 128:256] = sums[1][1] + sums[2][0]
        up_ref[here, 0:128] = sums[0][0].astype(BF16)
        up_ref[here, 128:256] = recv_refs[0][176 + 32 * g : 192 + 32 * g, :]
        down_ref[here, 256:384] = sums[2][1].astype(BF16)
        down_ref[here, 384:512] = recv_refs[0][192 + 32 * g : 208 + 32 * g, :]


def forward_kernel(slot_ref, part_ref, down_ref, weight_ref, *refs):
    *hid_refs, win_ref, block_ref = refs
    odd = down_ref[:, 128:256]
    win_ref[...] = part_ref[...]
    win_ref[0:80, 0:128] = from_left(odd.astype(F32)).astype(BF16)
    win_ref[80:160, 0:128] = down_ref[:, 0:128]
    win_ref[160:240, 0:128] = odd
    hidden = tn(weight_ref[...], win_ref[...]).astype(BF16)
    for p in range(8):
        for g in range(5):
            block_ref[p, 16 * g : 16 * g + 16, :] = hidden[128 * g + 16 * p : 128 * g + 16 * p + 16]
    for n, k in enumerate(ORDER):
        hid_refs[n][...] = block_ref[slot_ref[0] ^ k]


def middle_kernel(own_ref, down_ref, up_ref, *refs):
    *hid_refs, act_ref, share_ref = refs
    hidden = hid_refs[0][...].astype(F32)
    for n in range(1, 8):
        hidden = hidden + hid_refs[n][...].astype(F32)
    cumul = 0.5 * (1.0 + lax.erf(hidden * (1.0 / math.sqrt(2.0))))
    density = jnp.exp(-0.5 * hidden * hidden) * (1.0 / math.sqrt(2.0 * math.pi))
    act_ref[...] = (hidden * cumul).astype(BF16)
    slopes = cumul + hidden * density
    act_grad = own_ref[...] + jnp.concatenate(
        [down_ref[:, 256:384].astype(F32), up_ref[:, 0:128].astype(F32)], axis=1
    )
    share_ref[0:80, :] = (act_grad * slopes).astype(BF16)
    share_ref[80:160, 0:128] = down_ref[:, 384:512]
    share_ref[80:160, 128:256] = up_ref[:, 128:256]


def group_grad_kernel(act_ref, cot_ref, part_ref, edge_ref, inner_ref):
    rows = [act_ref[:, 128 * i : 128 * i + 128].astype(F32) for i in range(2)]
    moved = [[move(x).astype(BF16) for x in rows] for move in (from_left, lambda x: x, from_right)]
    edge_ref[...] = jnp.zeros((5, 256, 256), BF16)
    inner_ref[...] = jnp.zeros((5, 256, 256), BF16)
    for g in range(5):
        for u in range(3):
            for v in range(3):
                base = 80 + 16 * (3 * u + v)
                for i in range(2):
                    row = i + 1 - u
                    target_ref = inner_ref if 0 <= row < 2 else edge_ref
                    lanes = slice(0, 128) if row in (0, -1) else slice(128, 256)
                    target_ref[g, base : base + 16, lanes] = moved[v][i][16 * g : 16 * g + 16]
    for g in range(5):
        here = slice(128 * g, 128 * g + 128)
        part_ref[here, :] = nt(cot_ref[here, :], inner_ref[g])


def weight_grad_kernel(slot_ref, win_ref, part_ref, shift_ref, *refs):
    *all_refs, red_ref, pre_ref, cell_ref = refs
    for n, k in enumerate(GATHERED):
        start = pl.multiple_of(16 * (slot_ref[0] ^ k), 16)
        for g in range(5):
            pre_ref[pl.ds(128 * g + start, 16), :] = all_refs[n][16 * g : 16 * g + 16, :]
            for side in range(2):
                cell_ref[pl.ds(128 * side + start, 16), 128 * g : 128 * g + 128] = all_refs[n][
                    80 + 16 * g : 96 + 16 * g, 128 * side : 128 * side + 128
                ]
    pre = pre_ref[...]
    red_ref[:, 0:640] = nt(pre, win_ref[0:640, :]).astype(BF16)
    eye = jnp.where(iota((128, 128), 0) == iota((128, 128), 1), 1.0, 0.0).astype(BF16)
    tail = jnp.concatenate([win_ref[640:720, :], jnp.zeros((176, 256), BF16)], axis=0)
    last = nt(pre, tail)
    for g in range(5):
        here = slice(128 * g, 128 * g + 128)
        rims = nt(eye, cell_ref[:, here]).astype(BF16)
        group = part_ref[here, :] + nt(rims, shift_ref[g])
        red_ref[here, 640:896] = (last[here] + group).astype(BF16)


def image_grad_kernel(pre_ref, weight_ref, img_ref, up_ref):
    pre = pre_ref[...]
    back = nn(weight_ref[...], pre)

    def term(a, b, i):
        t = 3 * a + b
        return back[80 * t : 80 * t + 80, 128 * i : 128 * i + 128]

    for i in range(2):
        img_ref[4 * i] = term(1, 1, i)
        img_ref[4 * i + 1] = term(1, 2, i) + from_right(term(1, 0, i))
    upper_even = [term(0, 1, i) for i in range(2)]
    upper_odd = [term(0, 2, i) + from_right(term(0, 0, i)) for i in range(2)]
    lower_odd = [term(2, 2, i) + from_right(term(2, 0, i)) for i in range(2)]
    img_ref[2] = term(2, 1, 0) + upper_even[1]
    img_ref[3] = lower_odd[0] + upper_odd[1]
    img_ref[6] = term(2, 1, 1)
    img_ref[7] = lower_odd[1]
    up_ref[0] = upper_even[0].astype(BF16)
    up_ref[1] = upper_odd[0].astype(BF16)


def return_kernel(slot_ref, img_ref, below_ref, *refs):
    *send_refs, slot_blocks = refs
    parts = [img_ref[k] for k in range(8)]
    parts[6] = parts[6] + below_ref[0].astype(F32)
    parts[7] = parts[7] + below_ref[1].astype(F32)
    for q, x in enumerate(swap_blocks(parts)):
        slot_blocks[q] = x.astype(BF16)
    for n in range(5):
        send_refs[n][0:80, :] = slot_blocks[slot_ref[0] ^ SOURCE[n]]
        if 0 < n < 4:
            send_refs[n][80:160, :] = slot_blocks[slot_ref[0] ^ SOURCE[n] ^ 1]


def fold_kernel(high_ref, red_ref, keep_ref, give_ref):
    total = red_ref[0].astype(F32)
    for q in range(1, 16):
        total = total + red_ref[q].astype(F32)
    first, second = total[0:20], total[20:40]
    high = high_ref[0] == 1
    keep_ref[...] = jnp.where(high, second, first)
    give_ref[...] = jnp.where(high, first, second).astype(BF16)


def join_kernel(keep_ref, own_ref, *refs):
    *line_refs, out_ref = refs
    out_ref[0:80, :] = own_ref[...]
    for n, line_ref in enumerate(line_refs):
        out_ref[80 * n + 80 : 80 * n + 160, :] = line_ref[80:160, :]


def unpack_kernel(slot_ref, *refs):
    *recv_refs, joined_ref, out_ref, token_ref, block_ref = refs
    token_ref[...] = joined_ref[0:16, :]
    for n in range(4):
        block_ref[slot_ref[0] ^ SOURCE[n]] = recv_refs[n][0:80, :]
        block_ref[slot_ref[0] ^ SOURCE[n] ^ 1] = joined_ref[80 * n : 80 * n + 80, :]
    lane = iota((128, 128), 1)
    pick = jnp.where(cell_of_lane(lane) == iota((128, 128), 0), 1.0, 0.0).astype(BF16)
    blocks = block_ref[...].reshape(640, 128)
    for p in range(5):
        out_ref[:, 128 * p : 128 * p + 128] = nt(pick, blocks[128 * p : 128 * p + 128]).astype(BF16)


def finish_kernel(keep_ref, given_ref, token_ref, conv_ref, group_ref):
    total = keep_ref[...] + given_ref[...].astype(F32)
    for t in range(9):
        conv_ref[t] = total[:, 80 * t : 80 * t + 80]
    group_ref[...] = jnp.transpose(total[:, 640:896])[80:224]


def call(kernel, outs, *args, scratch=(), smem=0, flops=0):
    whole = [pl.BlockSpec(memory_space=pltpu.SMEM)] * smem
    whole += [pl.BlockSpec(memory_space=pltpu.VMEM)] * (len(args) - smem)
    return pl.pallas_call(
        kernel,
        out_shape=[jax.ShapeDtypeStruct(shape, dtype) for shape, dtype in outs],
        in_specs=whole,
        out_specs=[pl.BlockSpec(memory_space=pltpu.VMEM)] * len(outs),
        scratch_shapes=list(scratch),
        compiler_params=pltpu.CompilerParams(vmem_limit_bytes=48 * 1024 * 1024),
        cost_estimate=pl.CostEstimate(flops=flops, bytes_accessed=0, transcendentals=0) if flops else None,
    )(*args)


def swap(block, k):
    return lax.ppermute(block, "fsdp", [(i, i ^ k) for i in range(8)])


def exchange(blocks, source=SOURCE):
    direct = [swap(block, k) for block, k in zip(blocks[1:], source[1:5])]
    return [blocks[0]] + direct + [swap(got, 1) for got in direct[:3]]


def rows_for(n, height):
    return slice(height, 2 * height) if n > 4 else slice(0, height)


def per_device(image, conv_weight, group_weight, cotangent):
    tiles = lax.axis_size("tile")
    downward = [(i, i + 1) for i in range(tiles - 1)]
    upward = [(i + 1, i) for i in range(tiles - 1)]
    partners = [(i, i ^ 1) for i in range(tiles)]
    planes = [[2 * i + z for i in range(tiles // 2)] for z in range(2)]

    cells = cotangent.reshape(32, 640)
    slot = lax.axis_index("fsdp").astype(jnp.int32).reshape(1)
    weights = conv_weight.transpose(1, 0, 2).reshape(720, 640)
    parts = exchange(
        call(
            pack_kernel, [((height, 128), BF16) for height in (336, 512, 512, 512, 336)],
            slot, image.reshape(128, 640), group_weight.transpose(0, 2, 1), cells,
            scratch=[pltpu.VMEM((8, 176, 128), BF16)], smem=1,
        )
    )
    windows, down, up, own, cot = call(
        spread_kernel,
        [((720, 256), BF16), ((80, 512), BF16), ((80, 256), BF16), ((80, 256), F32), ((640, 256), BF16)],
        slot, *parts,
        scratch=[pltpu.VMEM((256, 640), BF16), pltpu.VMEM((640, 256), BF16), pltpu.VMEM((8, 336, 128), BF16)],
        smem=1,
    )
    down = lax.ppermute(down, "tile", downward)
    *hid, windows = call(
        forward_kernel, [((80, 256), BF16)] * 8 + [((720, 256), BF16)],
        slot, windows, down, weights,
        scratch=[pltpu.VMEM((8, 80, 256), BF16)], smem=1, flops=HEAVY,
    )
    hid = [hid[0]] + [swap(block, k) for k, block in zip(ORDER[1:], hid[1:])]
    up = lax.ppermute(up, "tile", upward)
    act, share = call(
        middle_kernel, [((80, 256), BF16), ((160, 256), BF16)], own, down, up, *hid
    )
    part, edge = call(
        group_grad_kernel, [((640, 256), F32), ((5, 256, 256), BF16)], act, cot,
        scratch=[pltpu.VMEM((5, 256, 256), BF16)],
    )
    red, pre = call(
        weight_grad_kernel,
        [((640, 896), BF16), ((640, 256), BF16)],
        slot, windows, part, edge, *exchange([share] * 5, GATHERED),
        scratch=[pltpu.VMEM((256, 640), BF16)], smem=1,
    )
    img, img_up = call(
        image_grad_kernel, [((8, 80, 128), F32), ((2, 80, 128), BF16)], pre, weights
    )
    img_below = lax.ppermute(img_up, "tile", upward)
    red = lax.all_to_all(
        red.reshape(16, 40, 896), "tile", 0, 0, tiled=True, axis_index_groups=planes
    )
    own, *others, core = call(
        return_kernel, [((height, 128), BF16) for height in HEIGHTS], slot, img, img_below,
        scratch=[pltpu.VMEM((8, 80, 128), BF16)], smem=1,
    )
    others = [swap(block, k) for block, k in zip(others, SOURCE[1:4])]
    high = (lax.axis_index("tile") % 2).astype(jnp.int32).reshape(1)
    keep, give = call(fold_kernel, [((20, 896), F32), ((20, 896), BF16)], high, red, smem=1)
    given = lax.ppermute(give, "tile", partners)
    (core,) = call(join_kernel, [((320, 128), BF16)], keep, core, *others)
    core = swap(core, 1)
    image_grad, token = call(
        unpack_kernel, [((128, 640), BF16), ((16, 128), BF16)], slot, own, *others, core,
        scratch=[pltpu.VMEM((8, 80, 128), BF16)], smem=1,
    )
    conv_weight_grad, group_weight_grad = call(
        finish_kernel, [((9, 20, 80), F32), ((144, 20), F32)], keep, given, token
    )
    conv_weight_grad = conv_weight_grad.transpose(2, 0, 1)
    group_weight_grad = group_weight_grad.reshape(9, 16, 20)
    return (image_grad.reshape(4, 32, 640), conv_weight_grad, group_weight_grad)


def solution(mesh):
    placed = (
        P("tile", "fsdp", None),
        P("fsdp", None, None),
        P(None, None, "fsdp"),
        P("tile", "fsdp", None),
    )
    return jax.shard_map(
        per_device,
        mesh=mesh,
        in_specs=placed,
        out_specs=(P("tile", "fsdp", None), P("fsdp", None, "tile"), P(None, "fsdp", "tile")),
        check_vma=False,
    )
```
